512 devices in a mesh: replica: 32 (over y, x_hi, core), shard: 16 (over x_lo, z).
Axes of the slice: x: 4 (x_hi: 2, x_lo: 2; x = x_hi * 2 + x_lo), y: 8, z: 8, core: 2. Of those that a mesh axis runs over, the one named last changes fastest.
Arguments:
- image: bfloat16 [512, 14, 14, 768], P(('replica', 'shard')), may hold values from -6 to 6
- upstream: bfloat16 [512, 14, 14, 768], P(('replica', 'shard')), may hold values from -0.75 to 0.75
- group_ids: int32 [512], P(('replica', 'shard')), may hold values from 0 to 3
- group_weights: float32 [4], replicated, may hold values from 0.2 to 5
- conv_kernel: bfloat16 [7, 7, 768], replicated, may hold values from -0.875 to 0.875
- norm_gain: float32 [768], replicated, may hold values from 0.1 to 1.9
- first_weight: bfloat16 [768, 3072], P(None, 'shard'), may hold values from -0.21875 to 0.21875
- first_bias: float32 [3072], P('shard'), may hold values from -3 to 3
- second_weight: bfloat16 [3072, 768], P('shard'), may hold values from -0.109375 to 0.109375
- layer_scale: float32 [768], replicated, may hold values from 0.3 to 3
Outputs:
- grad_input: bfloat16 [512, 14, 14, 768], P(('replica', 'shard'))
- grad_first: float32 [768, 3072], P(None, 'shard')
- grad_first_bias: float32 [3072], P('shard')
- grad_second: float32 [3072, 768], P('shard')
- grad_kernel: float32 [7, 7, 768], replicated
- grad_gain: float32 [768], replicated
- grad_scale: float32 [768], replicated
The draws below stay inside these ranges and needn't reach their ends.
All inputs are finite; a program needn't handle non-finite values.
Results may differ from the reference program's by a relative error of at most 0.009.
Values may be sent and summed in bfloat16 or wider, within the bound.
No kernel may reach another device: no remote copies, remote signals or barrier semaphores. Data moves between devices by JAX's collectives and lax.ppermute only.
A program may use at most 128 MiB of HBM per device.

```python
import math
import jax
import jax.numpy as jnp
from jax import lax

D = 768
FF = 3072
MAP_ROWS = 14
MAP_COLS = 14
GROUPS = 4
IMAGES = 512


def plant(drawn, key, least, top_value):
    index_at = [jax.random.randint(jax.random.fold_in(key, axis), (), 0, length) for axis, length in enumerate(drawn.shape)]
    main_axis = drawn.shape.index(max(drawn.shape))
    next_to = index_at[:main_axis] + [(index_at[main_axis] + 1) % drawn.shape[main_axis]] + index_at[main_axis + 1:]
    return drawn.at[tuple(index_at)].set(least).at[tuple(next_to)].set(top_value)


def levels(stream_key, dims, cuts, least, top_value):
    level, own = 1.0, jax.random.fold_in(stream_key, 6)
    for axis_at, parts in cuts:
        heights = jnp.exp(jax.random.uniform(jax.random.fold_in(own, axis_at), (parts,), jnp.float32, least / len(cuts), top_value / len(cuts)))
        level = level * jnp.repeat(heights, dims[axis_at] // parts).reshape([-1 if axis == axis_at else 1 for axis in range(len(dims))])
    return level


def scatter_about(stream_key, dims, scale, limit, cuts=(), held_as=jnp.bfloat16):
    array = scale * jax.random.normal(stream_key, dims, jnp.float32)
    if cuts:
        array = array * levels(stream_key, dims, cuts, -0.22, 0.18)
    return jnp.clip(array, -limit, limit).astype(held_as)


def setup_inputs(seed: int = 0) -> dict:
    keys = jax.random.split(jax.random.key(seed), 11)
    image = scatter_about(keys[0], (IMAGES, MAP_ROWS, MAP_COLS, D), 1.0, 6.0, ((0, 512),))
    upstream = scatter_about(keys[1], (IMAGES, MAP_ROWS, MAP_COLS, D), 0.125, 0.75, ((0, 512),))
    group_ids = plant(jax.random.randint(keys[2], (IMAGES,), 0, GROUPS), jax.random.fold_in(keys[2], 1), 0, GROUPS - 1).astype(jnp.int32)
    group_weights = jnp.clip(jnp.exp(jax.random.uniform(keys[3], (GROUPS,), jnp.float32, math.log(0.2), math.log(5.0))), 0.2, 5.0)
    conv_kernel = scatter_about(keys[4], (7, 7, D), 49 ** -0.5, 0.875)
    norm_gain = jnp.clip(1.0 + 0.18 * jax.random.normal(keys[5], (D,), jnp.float32), 0.1, 1.9)
    first_weight = scatter_about(keys[6], (D, FF), D ** -0.5, 0.21875, ((1, 16),))
    first_bias = scatter_about(keys[7], (FF,), 0.5, 3.0, ((0, 16),), jnp.float32)
    second_weight = scatter_about(keys[8], (FF, D), FF ** -0.5, 0.109375, ((0, 16),))
    layer_scale = jnp.clip(jnp.exp(jax.random.uniform(keys[9], (D,), jnp.float32, math.log(0.3), math.log(3.0))), 0.3, 3.0)
    return dict(image=image, upstream=upstream, group_ids=group_ids, group_weights=group_weights, conv_kernel=conv_kernel, norm_gain=norm_gain, first_weight=first_weight, first_bias=first_bias, second_weight=second_weight, layer_scale=layer_scale)


def depthwise(image_map, kernel):
    rows_map, cols_map = (image_map.shape[0], image_map.shape[1])
    padded = jnp.pad(image_map, ((3, 3), (3, 3), (0, 0)))
    output = jnp.zeros(image_map.shape, jnp.float32)
    for row_shift in range(7):
        for col_shift in range(7):
            output = output + padded[row_shift:row_shift + rows_map, col_shift:col_shift + cols_map] * kernel[row_shift, col_shift]
    return output

def depthwise_back(signal, image_map, kernel):
    rows_map, cols_map = (image_map.shape[0], image_map.shape[1])
    padded_grad = jnp.pad(signal, ((3, 3), (3, 3), (0, 0)))
    padded_map = jnp.pad(image_map, ((3, 3), (3, 3), (0, 0)))
    input_grad = jnp.zeros(image_map.shape, jnp.float32)
    kernel_rows = []
    for row_shift in range(7):
        for col_shift in range(7):
            input_grad = input_grad + padded_grad[6 - row_shift:6 - row_shift + rows_map, 6 - col_shift:6 - col_shift + cols_map] * kernel[row_shift, col_shift]
            kernel_rows.append(lax.optimization_barrier(jnp.sum(signal * padded_map[row_shift:row_shift + rows_map, col_shift:col_shift + cols_map], axis=(0, 1))))
    kernel_grad = jnp.stack(kernel_rows).reshape(7, 7, image_map.shape[2])
    return (input_grad, kernel_grad)

def standardize(convolved):
    centred = convolved - lax.optimization_barrier(jnp.mean(convolved, axis=-1, keepdims=True))
    inv_std = lax.rsqrt(lax.optimization_barrier(jnp.mean(centred * centred, axis=-1, keepdims=True)) + 1e-06)
    return (centred * inv_std, inv_std)

def gelu_value(value):
    return 0.5 * value * (1.0 + lax.erf(value * 0.7071067811865476))

def gelu_slope(value):
    return 0.5 * (1.0 + lax.erf(value * 0.7071067811865476)) + value * jnp.exp(-0.5 * value * value) * 0.3989422804014327

def reference(image, upstream, group_ids, group_weights, conv_kernel, norm_gain, first_weight, first_bias, second_weight, layer_scale):
    kernel = conv_kernel.astype(jnp.float32)
    labels = jnp.arange(GROUPS, dtype=jnp.int32)
    weights = lax.optimization_barrier(jnp.sum(jnp.where(group_ids[:, None] == labels[None, :], group_weights[None, :], 0.0), axis=1))
    weight_sum = jnp.sum(weights)
    factor = IMAGES / weight_sum
    pixels = MAP_ROWS * MAP_COLS

    def one_image(carry, inputs):
        image_map, upstream_map, own_weight = inputs
        sum_first, sum_bias, sum_second, sum_kernel, sum_gain, sum_scale = carry
        field_map = image_map.astype(jnp.float32)
        convolved = depthwise(field_map, kernel).reshape(pixels, D)
        centred, inv_std = standardize(convolved)
        normed = (centred * norm_gain).astype(jnp.bfloat16)
        preact = jnp.dot(normed, first_weight, preferred_element_type=jnp.float32) + first_bias
        activation = gelu_value(preact).astype(jnp.bfloat16)
        scaled = (own_weight * upstream_map.reshape(pixels, D).astype(jnp.float32)).astype(jnp.bfloat16)
        branch_grad = (scaled.astype(jnp.float32) * layer_scale).astype(jnp.bfloat16)
        branch = jnp.dot(activation, second_weight, preferred_element_type=jnp.float32)
        sum_scale = sum_scale + lax.optimization_barrier(jnp.sum(scaled.astype(jnp.float32) * branch, axis=0))
        sum_second = sum_second + jnp.dot(activation.T, branch_grad, preferred_element_type=jnp.float32)
        hidden_grad = jnp.dot(branch_grad, second_weight.T, preferred_element_type=jnp.float32)
        preact_grad = (hidden_grad * gelu_slope(preact)).astype(jnp.bfloat16)
        sum_bias = sum_bias + lax.optimization_barrier(jnp.sum(preact_grad.astype(jnp.float32), axis=0))
        sum_first = sum_first + jnp.dot(normed.T, preact_grad, preferred_element_type=jnp.float32)
        normed_grad = jnp.dot(preact_grad, first_weight.T, preferred_element_type=jnp.float32)
        sum_gain = sum_gain + lax.optimization_barrier(jnp.sum(normed_grad * centred, axis=0))
        gained = normed_grad * norm_gain
        conv_grad = inv_std * (gained - lax.optimization_barrier(jnp.mean(gained, axis=-1, keepdims=True)) - centred * lax.optimization_barrier(jnp.mean(gained * centred, axis=-1, keepdims=True)))
        map_grad, kernel_grad = depthwise_back(conv_grad.reshape(MAP_ROWS, MAP_COLS, D), field_map, kernel)
        sum_kernel = sum_kernel + kernel_grad
        grad_map = (factor * (scaled.astype(jnp.float32).reshape(MAP_ROWS, MAP_COLS, D) + map_grad)).astype(jnp.bfloat16)
        return ((sum_first, sum_bias, sum_second, sum_kernel, sum_gain, sum_scale), grad_map)
    start = (jnp.zeros((D, FF), jnp.float32), jnp.zeros((FF,), jnp.float32), jnp.zeros((FF, D), jnp.float32), jnp.zeros((7, 7, D), jnp.float32), jnp.zeros((D,), jnp.float32), jnp.zeros((D,), jnp.float32))
    sums, grad_input = lax.scan(one_image, start, (image, upstream, weights))
    sum_first, sum_bias, sum_second, sum_kernel, sum_gain, sum_scale = sums
    return (grad_input, factor * sum_first, factor * sum_bias, factor * sum_second, factor * sum_kernel, factor * sum_gain, factor * sum_scale)
```

```python
import jax
import jax.numpy as jnp
import numpy as np
from jax import lax
from jax.experimental import pallas as pl
from jax.experimental.pallas import tpu as pltpu
from jax.sharding import Mesh, PartitionSpec as P

F32 = jnp.float32
BF16 = jnp.bfloat16
ROWS = 14
COLS = 14
WIDE = 16
PIX = ROWS * WIDE
CH = 768
LANES = 128
BLOCKS = CH // LANES
OWN = 48
HID = 384
PACK = 112
REPLICA = ("y", "xh", "core")
SHARD = ("xl", "z")
RING = ("xh", "xl")
TEAM = ("xh", "core", "xl")
INTERPRET = False


def params(limit_mib, **more):
    return pltpu.CompilerParams(vmem_limit_bytes=limit_mib * 1024 * 1024, **more)


def nt(left, right):
    return lax.dot_general(left, right, (((1,), (1,)), ((), ())), preferred_element_type=F32)


def tn(left, right):
    return lax.dot_general(left, right, (((0,), (0,)), ((), ())), preferred_element_type=F32)


def whole():
    return pl.BlockSpec(memory_space=pltpu.VMEM)


def scalars():
    return pl.BlockSpec(memory_space=pltpu.SMEM)


def pack_kernel(place_ref, first_ref, bias_ref, second_ref, out_ref):
    block = place_ref[0]
    column = place_ref[1]
    row = lax.broadcasted_iota(jnp.int32, (OWN, 192), 0)
    lane = lax.broadcasted_iota(jnp.int32, (OWN, 192), 1)
    pick = (lane == row + block * OWN).astype(BF16)
    out_ref[0:OWN, :] = nt(pick, first_ref[...]).astype(BF16)
    out_ref[OWN : 2 * OWN, :] = jnp.dot(pick, second_ref[...], preferred_element_type=F32).astype(BF16)
    unit = lax.broadcasted_iota(jnp.int32, (192, HID), 0) - block * OWN
    spot = lax.broadcasted_iota(jnp.int32, (192, HID), 1) - column * OWN
    put = ((unit == spot) & (unit >= 0) & (unit < OWN)).astype(BF16)
    bias = jnp.broadcast_to(bias_ref[...], (16, 192))
    high = bias.astype(BF16)
    low = (bias - high.astype(F32)).astype(BF16)
    out_ref[2 * OWN : PACK, 0:HID] = jnp.dot(high, put, preferred_element_type=F32).astype(BF16)
    out_ref[2 * OWN : PACK, HID:CH] = jnp.dot(low, put, preferred_element_type=F32).astype(BF16)


def pack_weights(place, first_weight, first_bias, second_weight):
    return pl.pallas_call(
        pack_kernel,
        out_shape=jax.ShapeDtypeStruct((PACK, CH), BF16),
        in_specs=[scalars(), whole(), whole(), whole()],
        out_specs=whole(),
        compiler_params=params(16),
        interpret=INTERPRET,
        name="pack",
    )(place, first_weight, first_bias.reshape(1, 192), second_weight)


def taps_sum(padded_ref, kernel, flip):
    halves = []
    for half in range(2):
        total = jnp.zeros((7, WIDE, LANES), F32)
        for b in range(7):
            moved = padded_ref[half * 7 : half * 7 + 13, b : b + WIDE, :]
            for a in range(7):
                tap = (6 - a) * 7 + (6 - b) if flip else a * 7 + b
                total = total + moved[a : a + 7] * kernel[tap : tap + 1, :].reshape(1, 1, LANES)
        halves.append(total)
    return halves


def column_mask():
    return (lax.broadcasted_iota(jnp.int32, (ROWS, WIDE, LANES), 1) < COLS).astype(F32)


def forward_kernel(image_ref, kernel_ref, gain_ref, normed_ref, centred_ref, inv_ref, padded, conv):
    j = pl.program_id(0)

    @pl.when(j == 0)
    def _():
        padded[...] = jnp.zeros_like(padded)

    padded[3:17, 3:17, :] = image_ref[...].astype(F32)
    halves = taps_sum(padded, kernel_ref[...].astype(F32), False)
    conv[j, 0:7] = halves[0]
    conv[j, 7:14] = halves[1]

    @pl.when(j == BLOCKS - 1)
    def _():
        mask = column_mask()
        total = conv[0]
        for i in range(1, BLOCKS):
            total = total + conv[i]
        mean = jnp.sum(total, axis=-1, keepdims=True) * (1.0 / CH)
        square = jnp.zeros((ROWS, WIDE, LANES), F32)
        for i in range(BLOCKS):
            part = conv[i] - mean
            square = square + part * part
        inv = lax.rsqrt(jnp.sum(square, axis=-1, keepdims=True) * (1.0 / CH) + 1e-06)
        inv_ref[...] = jnp.broadcast_to(inv, (ROWS, WIDE, LANES))
        for i in range(BLOCKS):
            part = (conv[i] - mean) * inv * mask
            centred_ref[i] = part
            lanes = slice(i * LANES, (i + 1) * LANES)
            gain = gain_ref[:, lanes].reshape(1, 1, LANES)
            normed_ref[:, lanes] = (part * gain).reshape(PIX, LANES).astype(BF16)


def forward(image, kernel, gain):
    return pl.pallas_call(
        forward_kernel,
        grid=(BLOCKS,),
        out_shape=(
            jax.ShapeDtypeStruct((PIX, CH), BF16),
            jax.ShapeDtypeStruct((BLOCKS, ROWS, WIDE, LANES), F32),
            jax.ShapeDtypeStruct((ROWS, WIDE, LANES), F32),
        ),
        in_specs=[
            pl.BlockSpec((ROWS, COLS, LANES), lambda j: (0, 0, j)),
            pl.BlockSpec((49, LANES), lambda j: (0, j)),
            pl.BlockSpec((1, CH), lambda j: (0, 0)),
        ],
        out_specs=(
            pl.BlockSpec((PIX, CH), lambda j: (0, 0)),
            pl.BlockSpec((BLOCKS, ROWS, WIDE, LANES), lambda j: (0, 0, 0, 0)),
            pl.BlockSpec((ROWS, WIDE, LANES), lambda j: (0, 0, 0)),
        ),
        scratch_shapes=[
            pltpu.VMEM((20, 24, LANES), F32),
            pltpu.VMEM((BLOCKS, ROWS, WIDE, LANES), F32),
        ],
        compiler_params=params(24),
        interpret=INTERPRET,
        name="conv_norm",
    )(image, kernel, gain)


def hidden_kernel(*refs):
    normed = refs[0:8]
    scaled = refs[8:16]
    pack_ref, layer_ref = refs[16:18]
    mine_ref, other_ref, act_ref, grad_ref = refs[18:22]
    first = pack_ref[:, 0:OWN, :].reshape(HID, CH)
    second = pack_ref[:, OWN : 2 * OWN, :].reshape(HID, CH)
    bias = jnp.sum(pack_ref[:, 2 * OWN : PACK, :].astype(F32), axis=0)[0:1, :]
    bias = bias[:, 0:HID] + bias[:, HID:CH]
    layer = layer_ref[...]
    for i in range(8):
        preact = nt(normed[i][...], first) + bias
        cumulative = 0.5 * (1.0 + lax.erf(preact * 0.7071067811865476))
        slope = cumulative + preact * jnp.exp(-0.5 * preact * preact) * 0.3989422804014327
        act_ref[i] = (preact * cumulative).astype(BF16)
        branch_grad = (scaled[i][...].astype(F32) * layer).astype(BF16)
        preact_grad = (nt(branch_grad, second) * slope).astype(BF16)
        grad_ref[i] = preact_grad
        part = jnp.dot(preact_grad, first, preferred_element_type=F32).astype(BF16)
        if i % 2 == 0:
            mine_ref[i // 2] = part
        else:
            other_ref[i // 2] = part


def hidden(normed, scaled, pack, layer):
    return pl.pallas_call(
        hidden_kernel,
        out_shape=(
            jax.ShapeDtypeStruct((4, PIX, CH), BF16),
            jax.ShapeDtypeStruct((4, PIX, CH), BF16),
            jax.ShapeDtypeStruct((8, PIX, HID), BF16),
            jax.ShapeDtypeStruct((8, PIX, HID), BF16),
        ),
        in_specs=[whole()] * 18,
        out_specs=(whole(),) * 4,
        compiler_params=params(48),
        interpret=INTERPRET,
        name="hidden",
    )(*normed, *scaled, pack, layer)


def weights_kernel(*refs):
    normed = refs[0:8]
    scaled = refs[8:16]
    act_ref, grad_ref, pack_ref, layer_ref = refs[16:20]
    out_ref, scale_ref = refs[20:22]
    product = tn(act_ref[0], scaled[0][...])
    for i in range(1, 8):
        product = product + tn(act_ref[i], scaled[i][...])
    second = pack_ref[:, OWN : 2 * OWN, :].reshape(HID, CH).astype(F32)
    scale_ref[...] = jnp.sum((second * product).reshape(HID // 8, 8, CH), axis=0)
    spread(out_ref, (product * layer_ref[...]).astype(BF16), 0)
    product = tn(grad_ref[0], normed[0][...])
    for i in range(1, 8):
        product = product + tn(grad_ref[i], normed[i][...])
    spread(out_ref, product.astype(BF16), 18)
    ones = jnp.ones((16, PIX), BF16)
    bias = jnp.dot(ones, grad_ref[0], preferred_element_type=F32)
    for i in range(1, 8):
        bias = bias + jnp.dot(ones, grad_ref[i], preferred_element_type=F32)
    row = lax.broadcasted_iota(jnp.int32, (16, LANES), 0)
    block = jnp.zeros((16, LANES), F32)
    for k in range(3):
        block = jnp.where(row == k, bias[:, k * LANES : (k + 1) * LANES], block)
    block = block.astype(BF16)
    empty = jnp.zeros((16, LANES), BF16)
    for z in range(8):
        for s in range(36, 40):
            out_ref[(s // 5) * 8 + z, (s % 5) * 16 : (s % 5) * 16 + 16, :] = block if s == 36 else empty


def spread(out_ref, matrix, start):
    for z in range(8):
        for j in range(BLOCKS):
            for part in range(3):
                s = start + j * 3 + part
                row = z * OWN + part * 16
                out_ref[(s // 5) * 8 + z, (s % 5) * 16 : (s % 5) * 16 + 16, :] = matrix[
                    row : row + 16, j * LANES : (j + 1) * LANES
                ]


def weight_grads(normed, scaled, act, grad, pack, layer):
    return pl.pallas_call(
        weights_kernel,
        out_shape=(
            jax.ShapeDtypeStruct((64, 80, LANES), BF16),
            jax.ShapeDtypeStruct((8, CH), F32),
        ),
        in_specs=[whole()] * 20,
        out_specs=(whole(),) * 2,
        compiler_params=params(48),
        interpret=INTERPRET,
        name="weight_grads",
    )(*normed, *scaled, act, grad, pack, layer)


def pair_kernel(mine_ref, got_ref, *out_refs):
    for r in range(1, 4):
        out_refs[r - 1][...] = (mine_ref[r].astype(F32) + got_ref[r].astype(F32)).astype(BF16)


def pair_sums(mine, got):
    return pl.pallas_call(
        pair_kernel,
        out_shape=(jax.ShapeDtypeStruct((PIX, CH), BF16),) * 3,
        in_specs=[whole()] * 2,
        out_specs=(whole(),) * 3,
        compiler_params=params(24),
        interpret=INTERPRET,
        name="pair_sums",
    )(mine, got)


def backward_kernel(
    mine_ref, got_ref, one_ref, two_ref, three_ref, centred_ref, inv_ref, gain_ref, scale_ref, image_ref,
    sums_ref, conv_ref, padded, conv, parts, gains,
):
    j = pl.program_id(0)

    @pl.when(j == 0)
    def _():
        padded[...] = jnp.zeros_like(padded)
        first = jnp.zeros((ROWS, WIDE, LANES), F32)
        second = jnp.zeros((ROWS, WIDE, LANES), F32)
        for i in range(BLOCKS):
            lanes = slice(i * LANES, (i + 1) * LANES)
            grad = (
                mine_ref[0, :, lanes].astype(F32)
                + got_ref[0, :, lanes].astype(F32)
                + one_ref[:, lanes].astype(F32)
                + two_ref[:, lanes].astype(F32)
                + three_ref[:, lanes].astype(F32)
            ).reshape(ROWS, WIDE, LANES)
            centred = centred_ref[i]
            product = grad * centred
            gains[i] = jnp.sum(jnp.sum(product, axis=0).reshape(2, 8, LANES), axis=0)
            gain = gain_ref[:, lanes].reshape(1, 1, LANES)
            gained = grad * gain
            conv[i] = gained
            first = first + gained
            second = second + product * gain
        mean = jnp.sum(first, axis=-1, keepdims=True) * (1.0 / CH)
        slant = jnp.sum(second, axis=-1, keepdims=True) * (1.0 / CH)
        inv = inv_ref[...] * column_mask()
        for i in range(BLOCKS):
            conv[i] = inv * (conv[i] - mean - centred_ref[i] * slant)

    padded[3:17, 3:17, :] = image_ref[...].astype(F32)
    conv_ref[0] = conv[j]
    for half in range(2):
        signal = conv[j, half * 7 : half * 7 + 7]
        for b in range(7):
            moved = padded[half * 7 : half * 7 + 13, b : b + WIDE, :]
            for a in range(7):
                product = jnp.sum(signal * moved[a : a + 7], axis=0)
                product = product[0:8] + product[8:16]
                if half == 0:
                    parts[a * 7 + b] = product
                else:
                    parts[a * 7 + b] += product
    sums_ref[0] = jnp.zeros((64, LANES), F32)
    sums_ref[0, 0:49, :] = jnp.sum(parts[...], axis=1)
    sums_ref[0, 49:50, :] = jnp.sum(gains[j], axis=0, keepdims=True)
    sums_ref[0, 50:51, :] = jnp.sum(scale_ref[...], axis=0, keepdims=True)


def backward(mine, got, one, two, three, centred, inv, gain, scale, image):
    def fixed(*shape):
        return pl.BlockSpec(shape, lambda j: (0,) * len(shape))

    return pl.pallas_call(
        backward_kernel,
        grid=(BLOCKS,),
        out_shape=(
            jax.ShapeDtypeStruct((BLOCKS, 64, LANES), F32),
            jax.ShapeDtypeStruct((BLOCKS, ROWS, WIDE, LANES), F32),
        ),
        in_specs=[
            fixed(1, PIX, CH),
            fixed(1, PIX, CH),
            fixed(PIX, CH),
            fixed(PIX, CH),
            fixed(PIX, CH),
            fixed(BLOCKS, ROWS, WIDE, LANES),
            fixed(ROWS, WIDE, LANES),
            fixed(1, CH),
            pl.BlockSpec((8, LANES), lambda j: (0, j)),
            pl.BlockSpec((ROWS, COLS, LANES), lambda j: (0, 0, j)),
        ],
        out_specs=(
            pl.BlockSpec((1, 64, LANES), lambda j: (j, 0, 0)),
            pl.BlockSpec((1, ROWS, WIDE, LANES), lambda j: (j, 0, 0, 0)),
        ),
        scratch_shapes=[
            pltpu.VMEM((20, 24, LANES), F32),
            pltpu.VMEM((BLOCKS, ROWS, WIDE, LANES), F32),
            pltpu.VMEM((49, 8, LANES), F32),
            pltpu.VMEM((BLOCKS, 8, LANES), F32),
        ],
        compiler_params=params(32),
        interpret=INTERPRET,
        name="norm_back",
    )(mine, got, one, two, three, centred, inv, gain, scale, image)


def input_kernel(factor_ref, conv_ref, kernel_ref, scaled_ref, out_ref, padded):
    @pl.when(pl.program_id(0) == 0)
    def _():
        padded[...] = jnp.zeros_like(padded)

    padded[3:17, 3 : 3 + WIDE, :] = conv_ref[0]
    halves = taps_sum(padded, kernel_ref[...].astype(F32), True)
    factor = factor_ref[0]
    for half in range(2):
        rows = slice(half * 7 * WIDE, (half + 1) * 7 * WIDE)
        scaled = scaled_ref[rows, :].astype(F32).reshape(7, WIDE, LANES)
        result = (factor * (scaled + halves[half])).astype(BF16)
        out_ref[0, half * 7 : half * 7 + 7] = result[:, 0:COLS, :]


def input_grad(factor, conv, kernel, scaled):
    return pl.pallas_call(
        input_kernel,
        grid=(BLOCKS,),
        out_shape=jax.ShapeDtypeStruct((1, ROWS, COLS, CH), BF16),
        in_specs=[
            scalars(),
            pl.BlockSpec((1, ROWS, WIDE, LANES), lambda j: (j, 0, 0, 0)),
            pl.BlockSpec((49, LANES), lambda j: (0, j)),
            pl.BlockSpec((PIX, LANES), lambda j: (0, j)),
        ],
        out_specs=pl.BlockSpec((1, ROWS, COLS, LANES), lambda j: (0, 0, 0, j)),
        scratch_shapes=[pltpu.VMEM((20, 24, LANES), F32)],
        compiler_params=params(24),
        interpret=INTERPRET,
        name="input_grad",
    )(factor, conv, kernel, scaled)


def unpack_kernel(factor_ref, core_ref, mine_ref, other_ref, first_ref, second_ref):
    factor = factor_ref[0]
    even = core_ref[0] == 0

    def column(kind, j):
        pieces = []
        for xh in range(2):
            own, got = [], []
            for part in range(3):
                s = kind * 18 + j * 3 + part
                rows = slice((s % 5) * 16, (s % 5) * 16 + 16)
                own.append(mine_ref[(s // 5) * 2 + xh, rows, :].astype(F32))
                got.append(other_ref[(s // 5) * 2 + xh, rows, :].astype(F32))
            own, got = jnp.concatenate(own), jnp.concatenate(got)
            pieces += [jnp.where(even, own, got), jnp.where(even, got, own)]
        return jnp.concatenate(pieces) * factor

    for j in range(BLOCKS):
        lanes = slice(j * LANES, (j + 1) * LANES)
        second_ref[:, lanes] = column(0, j)
        first_ref[lanes, :] = column(1, j).T


def unpack(factor, core, mine, other):
    return pl.pallas_call(
        unpack_kernel,
        out_shape=(
            jax.ShapeDtypeStruct((CH, 192), F32),
            jax.ShapeDtypeStruct((192, CH), F32),
        ),
        in_specs=[scalars(), scalars(), whole(), whole()],
        out_specs=(whole(),) * 2,
        compiler_params=params(16),
        interpret=INTERPRET,
        name="unpack",
    )(factor, core, mine, other)


def to_all(value, axes):
    count = lax.axis_size(axes)
    return lax.all_to_all(jnp.broadcast_to(value, (count, *value.shape)), axes, 0, 0, tiled=True)


def swap_core(value):
    return lax.ppermute(value, "core", [(0, 1), (1, 0)])


def ring(value, shift):
    return lax.ppermute(value, RING, [(i, (i + shift) % 4) for i in range(4)])


def share(value):
    mine = [value] + [ring(value, r) for r in range(1, 4)]
    result = []
    for item in mine:
        result += [item, swap_core(item)]
    return result


def per_device(
    image, upstream, group_ids, group_weights, conv_kernel, norm_gain, first_weight, first_bias, second_weight, layer_scale
):
    core = lax.axis_index("core")
    block = lax.axis_index("xh") * 2 + core
    column = lax.axis_index("z")
    place = jnp.stack([block, column]).astype(jnp.int32)
    packed = pack_weights(place, first_weight, first_bias, second_weight)
    packed = lax.all_gather(packed, "z", axis=0, tiled=True).reshape(8, PACK, CH)

    labels = jnp.arange(group_weights.shape[0], dtype=jnp.int32)
    own_weight = jnp.sum(jnp.where(labels == group_ids[0], group_weights, 0.0))
    scaled = (own_weight * upstream[0].astype(F32)).astype(BF16)
    scaled = jnp.pad(scaled, ((0, 0), (0, WIDE - COLS), (0, 0))).reshape(PIX, CH)
    scaled_all = share(scaled)

    kernel = conv_kernel.reshape(49, CH)
    gain = norm_gain.reshape(1, CH)
    layer = layer_scale.reshape(1, CH)
    normed, centred, inv = forward(image[0], kernel, gain)
    normed_all = share(normed)

    weight_sum = jnp.sum(to_all(jnp.full((8, LANES), own_weight, F32), SHARD), axis=0)
    weight_sum = jnp.sum(to_all(weight_sum, REPLICA), axis=0)
    images = lax.axis_size(REPLICA) * lax.axis_size(SHARD)
    factor = (images / weight_sum[0:1, 0]).astype(F32)

    mine, other, act, preact_grad = hidden(normed_all, scaled_all, packed, layer)
    got = swap_core(other)
    sums = pair_sums(mine, got)
    returned = [ring(sums[r - 1], 4 - r) for r in range(1, 4)]

    grads, scale = weight_grads(normed_all, scaled_all, act, preact_grad, packed, layer)
    grads = lax.all_to_all(grads, ("y", "z"), 0, 0, tiled=True)
    grads = jnp.sum(grads.astype(F32), axis=0).astype(BF16)
    grads = to_all(grads, ("y", "xh"))
    grads_other = swap_core(grads)
    grad_first, grad_second = unpack(factor, core.reshape(1).astype(jnp.int32), grads, grads_other)

    def bias_of(gathered):
        both = gathered[14:16, 16:32, :][:, 0:3, :].reshape(2, HID).astype(F32)
        return lax.dynamic_slice(both, (0, column * OWN), (2, OWN))

    bias_mine, bias_other = bias_of(grads), bias_of(grads_other)
    bias = jnp.stack([jnp.where(core == 0, bias_mine, bias_other), jnp.where(core == 0, bias_other, bias_mine)], axis=1)
    grad_bias = factor * bias.reshape(4 * OWN)

    small, conv_grad = backward(mine, got, *returned, centred, inv, gain, scale, image[0])
    small = lax.all_to_all(small.reshape(8, OWN, LANES), TEAM, 0, 0, tiled=True)
    small = jnp.sum(small, axis=0)
    small = jnp.sum(to_all(small, "y"), axis=0)
    small = jnp.sum(to_all(small, "z"), axis=0)
    small = to_all(small, TEAM).reshape(BLOCKS, 64, LANES) * factor
    small = small.transpose(1, 0, 2).reshape(64, CH)
    grad_image = input_grad(factor, conv_grad, kernel, scaled)
    return (
        grad_image,
        grad_first,
        grad_bias,
        grad_second,
        small[0:49].reshape(7, 7, CH),
        small[49],
        small[50],
    )


def solution(mesh):
    fine = Mesh(mesh.devices.reshape(8, 2, 2, 2, 8), ("y", "xh", "core", "xl", "z"))
    images = P((*REPLICA, *SHARD), None, None, None)
    return jax.shard_map(
        per_device,
        mesh=fine,
        in_specs=(
            images,
            images,
            P((*REPLICA, *SHARD)),
            P(),
            P(),
            P(),
            P(None, SHARD),
            P(SHARD),
            P(SHARD, None),
            P(),
        ),
        out_specs=(images, P(None, SHARD), P(SHARD), P(SHARD, None), P(), P(), P()),
        check_vma=False,
    )
```

```python
import jax
import jax.numpy as jnp
import numpy as np
from jax import lax
from jax.experimental import pallas as pl
from jax.experimental.pallas import tpu as pltpu
from jax.sharding import Mesh, PartitionSpec as P

F32 = jnp.float32
BF16 = jnp.bfloat16
ROWS = 14
COLS = 14
WIDE = 16
PIX = ROWS * WIDE
CH = 768
LANES = 128
BLOCKS = CH // LANES
OWN = 48
HALF = 384
PACK = 64
REPLICA = ("y", "xh", "core")
SHARD = ("xl", "z")
RING = ("xh", "xl")
TEAM = ("core", "xl", "xh")
INTERPRET = False


def params(limit_mib, **more):
    return pltpu.CompilerParams(vmem_limit_bytes=limit_mib * 1024 * 1024, **more)


def nt(left, right):
    return lax.dot_general(left, right, (((1,), (1,)), ((), ())), preferred_element_type=F32)


def tn(left, right):
    return lax.dot_general(left, right, (((0,), (0,)), ((), ())), preferred_element_type=F32)


def whole():
    return pl.BlockSpec(memory_space=pltpu.VMEM)


def scalars():
    return pl.BlockSpec(memory_space=pltpu.SMEM)


def pack_kernel(place_ref, first_ref, bias_ref, second_ref, one_ref, two_ref):
    block = place_ref[0]
    column = place_ref[1]
    row = lax.broadcasted_iota(jnp.int32, (2 * OWN, 192), 0)
    lane = lax.broadcasted_iota(jnp.int32, (2 * OWN, 192), 1)
    partner = block + 1 - 2 * lax.rem(block, 2)
    wanted = jnp.where(row < OWN, row + block * OWN, row - OWN + partner * OWN)
    pick = (lane == wanted).astype(BF16)
    one_ref[0:OWN, :] = nt(pick[0:OWN], first_ref[...]).astype(BF16)
    two_ref[...] = jnp.dot(pick, second_ref[...], preferred_element_type=F32).astype(BF16)
    unit = lax.broadcasted_iota(jnp.int32, (192, HALF), 0) - block * OWN
    spot = lax.broadcasted_iota(jnp.int32, (192, HALF), 1) - column * OWN
    put = ((unit == spot) & (unit >= 0) & (unit < OWN)).astype(BF16)
    bias = jnp.broadcast_to(bias_ref[...], (16, 192))
    high = bias.astype(BF16)
    low = (bias - high.astype(F32)).astype(BF16)
    one_ref[OWN:PACK, 0:HALF] = jnp.dot(high, put, preferred_element_type=F32).astype(BF16)
    one_ref[OWN:PACK, HALF:CH] = jnp.dot(low, put, preferred_element_type=F32).astype(BF16)


def pack_weights(place, first_weight, first_bias, second_weight):
    return pl.pallas_call(
        pack_kernel,
        out_shape=(jax.ShapeDtypeStruct((PACK, CH), BF16), jax.ShapeDtypeStruct((2 * OWN, CH), BF16)),
        in_specs=[scalars(), whole(), whole(), whole()],
        out_specs=(whole(), whole()),
        compiler_params=params(8),
        interpret=INTERPRET,
        name="pack",
    )(place, first_weight, first_bias.reshape(1, 192), second_weight)


def taps_sum(padded_ref, kernel, flip):
    halves = []
    for half in range(2):
        total = jnp.zeros((7, WIDE, LANES), F32)
        for b in range(7):
            moved = padded_ref[half * 7 : half * 7 + 13, b : b + WIDE, :]
            for a in range(7):
                tap = (6 - a) * 7 + (6 - b) if flip else a * 7 + b
                total = total + moved[a : a + 7] * kernel[tap : tap + 1, :].reshape(1, 1, LANES)
        halves.append(total)
    return halves


def column_mask():
    return (lax.broadcasted_iota(jnp.int32, (ROWS, WIDE, LANES), 1) < COLS).astype(F32)


def forward_kernel(image_ref, kernel_ref, gain_ref, normed_ref, centred_ref, inv_ref, padded, conv):
    j = pl.program_id(0)

    @pl.when(j == 0)
    def _():
        padded[...] = jnp.zeros_like(padded)

    padded[3:17, 3:17, :] = image_ref[...].astype(F32)
    halves = taps_sum(padded, kernel_ref[...].astype(F32), False)
    conv[j, 0:7] = halves[0]
    conv[j, 7:14] = halves[1]

    @pl.when(j == BLOCKS - 1)
    def _():
        mask = column_mask()
        total = conv[0]
        for i in range(1, BLOCKS):
            total = total + conv[i]
        mean = jnp.sum(total, axis=-1, keepdims=True) * (1.0 / CH)
        square = jnp.zeros((ROWS, WIDE, LANES), F32)
        for i in range(BLOCKS):
            part = conv[i] - mean
            square = square + part * part
        inv = lax.rsqrt(jnp.sum(square, axis=-1, keepdims=True) * (1.0 / CH) + 1e-06)
        inv_ref[...] = jnp.broadcast_to(inv, (ROWS, WIDE, LANES))
        for i in range(BLOCKS):
            part = (conv[i] - mean) * inv * mask
            centred_ref[i] = part
            lanes = slice(i * LANES, (i + 1) * LANES)
            gain = gain_ref[:, lanes].reshape(1, 1, LANES)
            normed_ref[:, lanes] = (part * gain).reshape(PIX, LANES).astype(BF16)


def forward(image, kernel, gain):
    return pl.pallas_call(
        forward_kernel,
        grid=(BLOCKS,),
        out_shape=(
            jax.ShapeDtypeStruct((PIX, CH), BF16),
            jax.ShapeDtypeStruct((BLOCKS, ROWS, WIDE, LANES), F32),
            jax.ShapeDtypeStruct((ROWS, WIDE, LANES), F32),
        ),
        in_specs=[
            pl.BlockSpec((ROWS, COLS, LANES), lambda j: (0, 0, j)),
            pl.BlockSpec((49, LANES), lambda j: (0, j)),
            pl.BlockSpec((1, CH), lambda j: (0, 0)),
        ],
        out_specs=(
            pl.BlockSpec((PIX, CH), lambda j: (0, 0)),
            pl.BlockSpec((BLOCKS, ROWS, WIDE, LANES), lambda j: (0, 0, 0, 0)),
            pl.BlockSpec((ROWS, WIDE, LANES), lambda j: (0, 0, 0)),
        ),
        scratch_shapes=[
            pltpu.VMEM((20, 24, LANES), F32),
            pltpu.VMEM((BLOCKS, ROWS, WIDE, LANES), F32),
        ],
        compiler_params=params(24),
        interpret=INTERPRET,
        name="conv_norm",
    )(image, kernel, gain)


def first_of(mine_ref, other_ref):
    return jnp.concatenate(
        [ref[:, 0:OWN, :].reshape(HALF, CH) for ref in (mine_ref, other_ref)], axis=0
    )


def second_of(two_ref):
    return jnp.concatenate(
        [two_ref[:, k * OWN : (k + 1) * OWN, :].reshape(HALF, CH) for k in range(2)], axis=0
    )


def activation_kernel(*refs):
    normed = refs[0:4]
    mine_ref, other_ref, act_ref, slope_ref = refs[4:8]
    first = first_of(mine_ref, other_ref)
    biases = []
    for ref in (mine_ref, other_ref):
        bias = jnp.sum(ref[:, OWN:PACK, :].astype(F32), axis=0)[0:1, :]
        biases.append(bias[:, 0:HALF] + bias[:, HALF:CH])
    bias = jnp.concatenate(biases, axis=1)
    for i in range(4):
        preact = nt(normed[i][...], first) + bias
        cumulative = 0.5 * (1.0 + lax.erf(preact * 0.7071067811865476))
        slope_ref[i] = cumulative + preact * jnp.exp(-0.5 * preact * preact) * 0.3989422804014327
        act_ref[i] = (preact * cumulative).astype(BF16)


def activations(normed, mine, other):
    return pl.pallas_call(
        activation_kernel,
        out_shape=(
            jax.ShapeDtypeStruct((4, PIX, CH), BF16),
            jax.ShapeDtypeStruct((4, PIX, CH), F32),
        ),
        in_specs=[whole()] * 6,
        out_specs=(whole(),) * 2,
        compiler_params=params(16),
        interpret=INTERPRET,
        name="activations",
    )(*normed, mine, other)


def hidden_kernel(*refs):
    scaled = refs[0:4]
    mine_ref, other_ref, two_ref, layer_ref, slope_ref = refs[4:9]
    grad_ref = refs[9]
    parts = refs[10:14]
    first = first_of(mine_ref, other_ref)
    second = second_of(two_ref)
    layer = layer_ref[...]
    for i in (2, 1, 3, 0):
        branch_grad = (scaled[i][...].astype(F32) * layer).astype(BF16)
        preact_grad = (nt(branch_grad, second) * slope_ref[i]).astype(BF16)
        grad_ref[i] = preact_grad
        parts[i][...] = jnp.dot(preact_grad, first, preferred_element_type=F32).astype(BF16)


def hidden(scaled, mine, other, two, layer, slope):
    return pl.pallas_call(
        hidden_kernel,
        out_shape=(jax.ShapeDtypeStruct((4, PIX, CH), BF16),)
        + (jax.ShapeDtypeStruct((PIX, CH), BF16),) * 4,
        in_specs=[whole()] * 9,
        out_specs=(whole(),) * 5,
        compiler_params=params(16),
        interpret=INTERPRET,
        name="hidden",
    )(*scaled, mine, other, two, layer, slope)


def weights_kernel(*refs):
    normed = refs[0:4]
    scaled = refs[4:8]
    act_ref, grad_ref, two_ref, layer_ref = refs[8:12]
    outs = refs[12:14]
    scale_ref = refs[14]
    product = tn(
        act_ref[...].reshape(4 * PIX, CH), jnp.concatenate([ref[...] for ref in scaled], axis=0)
    )
    weighted = second_of(two_ref).astype(F32) * product
    scale_ref[...] = jnp.sum(weighted.reshape(CH // 8, 8, CH), axis=0)
    product = (product * layer_ref[...]).astype(BF16)
    for half in range(2):
        spread(outs[half], product[half * HALF : (half + 1) * HALF], 0)
    product = tn(
        grad_ref[...].reshape(4 * PIX, CH), jnp.concatenate([ref[...] for ref in normed], axis=0)
    ).astype(BF16)
    for half in range(2):
        spread(outs[half], product[half * HALF : (half + 1) * HALF], 18)
    ones = jnp.ones((16, 4 * PIX), BF16)
    bias = jnp.dot(ones, grad_ref[...].reshape(4 * PIX, CH), preferred_element_type=F32)
    row = lax.broadcasted_iota(jnp.int32, (16, LANES), 0)
    empty = jnp.zeros((16, LANES), BF16)
    for half in range(2):
        block = jnp.zeros((16, LANES), F32)
        for k in range(3):
            start = half * HALF + k * LANES
            block = jnp.where(row == k, bias[:, start : start + LANES], block)
        block = block.astype(BF16)
        for z in range(8):
            for s in range(36, 40):
                outs[half][(s // 5) * 8 + z, (s % 5) * 16 : (s % 5) * 16 + 16, :] = block if s == 36 else empty


def spread(out_ref, matrix, start):
    for z in range(8):
        for j in range(BLOCKS):
            for part in range(3):
                s = start + j * 3 + part
                row = z * OWN + part * 16
                out_ref[(s // 5) * 8 + z, (s % 5) * 16 : (s % 5) * 16 + 16, :] = matrix[
                    row : row + 16, j * LANES : (j + 1) * LANES
                ]


def weight_grads(normed, scaled, act, grad, two, layer):
    return pl.pallas_call(
        weights_kernel,
        out_shape=(
            jax.ShapeDtypeStruct((64, 80, LANES), BF16),
            jax.ShapeDtypeStruct((64, 80, LANES), BF16),
            jax.ShapeDtypeStruct((8, CH), F32),
        ),
        in_specs=[whole()] * 12,
        out_specs=(whole(),) * 3,
        compiler_params=params(24),
        interpret=INTERPRET,
        name="weight_grads",
    )(*normed, *scaled, act, grad, two, layer)


def backward_kernel(
    weight_ref, zero_ref, one_ref, two_ref, three_ref, centred_ref, inv_ref, gain_ref, scale_ref, image_ref,
    sums_ref, conv_ref, padded, conv, parts, gains,
):
    j = pl.program_id(0)

    @pl.when(j == 0)
    def _():
        padded[...] = jnp.zeros_like(padded)
        first = jnp.zeros((ROWS, WIDE, LANES), F32)
        second = jnp.zeros((ROWS, WIDE, LANES), F32)
        for i in range(BLOCKS):
            lanes = slice(i * LANES, (i + 1) * LANES)
            grad = (
                zero_ref[:, lanes].astype(F32)
                + one_ref[:, lanes].astype(F32)
                + two_ref[:, lanes].astype(F32)
                + three_ref[:, lanes].astype(F32)
            ).reshape(ROWS, WIDE, LANES)
            centred = centred_ref[i]
            product = grad * centred
            gains[i] = jnp.sum(jnp.sum(product, axis=0).reshape(2, 8, LANES), axis=0)
            gain = gain_ref[:, lanes].reshape(1, 1, LANES)
            gained = grad * gain
            conv[i] = gained
            first = first + gained
            second = second + product * gain
        mean = jnp.sum(first, axis=-1, keepdims=True) * (1.0 / CH)
        slant = jnp.sum(second, axis=-1, keepdims=True) * (1.0 / CH)
        inv = inv_ref[...] * column_mask()
        for i in range(BLOCKS):
            conv[i] = inv * (conv[i] - mean - centred_ref[i] * slant)

    padded[3:17, 3:17, :] = image_ref[...].astype(F32)
    conv_ref[0] = conv[j]
    for half in range(2):
        signal = conv[j, half * 7 : half * 7 + 7]
        for b in range(7):
            moved = padded[half * 7 : half * 7 + 13, b : b + WIDE, :]
            for a in range(7):
                product = jnp.sum(signal * moved[a : a + 7], axis=0)
                product = product[0:8] + product[8:16]
                if half == 0:
                    parts[a * 7 + b] = product
                else:
                    parts[a * 7 + b] += product
    sums_ref[0] = jnp.zeros((64, LANES), F32)
    sums_ref[0, 0:49, :] = jnp.sum(parts[...], axis=1)
    sums_ref[0, 49:50, :] = jnp.sum(gains[j], axis=0, keepdims=True)
    sums_ref[0, 50:51, :] = jnp.sum(scale_ref[...], axis=0, keepdims=True)
    sums_ref[0, 51:52, :] = jnp.full((1, LANES), weight_ref[0], F32)


def backward(weight, zero, one, two, three, centred, inv, gain, scale, image):
    def fixed(*shape):
        return pl.BlockSpec(shape, lambda j: (0,) * len(shape))

    return pl.pallas_call(
        backward_kernel,
        grid=(BLOCKS,),
        out_shape=(
            jax.ShapeDtypeStruct((BLOCKS, 64, LANES), F32),
            jax.ShapeDtypeStruct((BLOCKS, ROWS, WIDE, LANES), F32),
        ),
        in_specs=[
            scalars(),
            fixed(PIX, CH),
            fixed(PIX, CH),
            fixed(PIX, CH),
            fixed(PIX, CH),
            fixed(BLOCKS, ROWS, WIDE, LANES),
            fixed(ROWS, WIDE, LANES),
            fixed(1, CH),
            pl.BlockSpec((8, LANES), lambda j: (0, j)),
            pl.BlockSpec((ROWS, COLS, LANES), lambda j: (0, 0, j)),
        ],
        out_specs=(
            pl.BlockSpec((1, 64, LANES), lambda j: (j, 0, 0)),
            pl.BlockSpec((1, ROWS, WIDE, LANES), lambda j: (j, 0, 0, 0)),
        ),
        scratch_shapes=[
            pltpu.VMEM((20, 24, LANES), F32),
            pltpu.VMEM((BLOCKS, ROWS, WIDE, LANES), F32),
            pltpu.VMEM((49, 8, LANES), F32),
            pltpu.VMEM((BLOCKS, 8, LANES), F32),
        ],
        compiler_params=params(32),
        interpret=INTERPRET,
        name="norm_back",
    )(weight, zero, one, two, three, centred, inv, gain, scale, image)


def input_kernel(conv_ref, kernel_ref, scaled_ref, out_ref, padded):
    @pl.when(pl.program_id(0) == 0)
    def _():
        padded[...] = jnp.zeros_like(padded)

    padded[3:17, 3 : 3 + WIDE, :] = conv_ref[0]
    halves = taps_sum(padded, kernel_ref[...].astype(F32), True)
    for half in range(2):
        rows = slice(half * 7 * WIDE, (half + 1) * 7 * WIDE)
        scaled = scaled_ref[rows, :].astype(F32).reshape(7, WIDE, LANES)
        out_ref[0, half * 7 : half * 7 + 7] = (scaled + halves[half])[:, 0:COLS, :]


def input_grad(conv, kernel, scaled):
    return pl.pallas_call(
        input_kernel,
        grid=(BLOCKS,),
        out_shape=jax.ShapeDtypeStruct((1, ROWS, COLS, CH), F32),
        in_specs=[
            pl.BlockSpec((1, ROWS, WIDE, LANES), lambda j: (j, 0, 0, 0)),
            pl.BlockSpec((49, LANES), lambda j: (0, j)),
            pl.BlockSpec((PIX, LANES), lambda j: (0, j)),
        ],
        out_specs=pl.BlockSpec((1, ROWS, COLS, LANES), lambda j: (0, 0, 0, j)),
        scratch_shapes=[pltpu.VMEM((20, 24, LANES), F32)],
        compiler_params=params(24),
        interpret=INTERPRET,
        name="input_grad",
    )(conv, kernel, scaled)


def unpack_kernel(factor_ref, core_ref, mine_ref, other_ref, first_ref, second_ref):
    factor = factor_ref[0]
    even = core_ref[0] == 0

    def column(kind, j):
        pieces = []
        for xh in range(2):
            own, got = [], []
            for part in range(3):
                s = kind * 18 + j * 3 + part
                rows = slice((s % 5) * 16, (s % 5) * 16 + 16)
                own.append(mine_ref[xh, s // 5, rows, :].astype(F32))
                got.append(other_ref[xh, s // 5, rows, :].astype(F32))
            own, got = jnp.concatenate(own), jnp.concatenate(got)
            pieces += [jnp.where(even, own, got), jnp.where(even, got, own)]
        return jnp.concatenate(pieces) * factor

    for j in range(BLOCKS):
        lanes = slice(j * LANES, (j + 1) * LANES)
        second_ref[:, lanes] = column(0, j)
        first_ref[lanes, :] = column(1, j).T


def unpack(factor, core, mine, other):
    return pl.pallas_call(
        unpack_kernel,
        out_shape=(
            jax.ShapeDtypeStruct((CH, 192), F32),
            jax.ShapeDtypeStruct((192, CH), F32),
        ),
        in_specs=[scalars(), scalars(), whole(), whole()],
        out_specs=(whole(),) * 2,
        compiler_params=params(16),
        interpret=INTERPRET,
        name="unpack",
    )(factor, core, mine, other)


def to_all(value, axes):
    count = lax.axis_size(axes)
    return lax.all_to_all(jnp.broadcast_to(value, (count, *value.shape)), axes, 0, 0, tiled=True)


def swap_core(value):
    return lax.ppermute(value, "core", [(0, 1), (1, 0)])


def ring(value, shift):
    return lax.ppermute(value, RING, [(i, (i + shift) % 4) for i in range(4)])


def ring_share(value):
    return [value] + [ring(value, r) for r in range(1, 4)]


def halve(value, axis):
    at = lax.axis_index(axis)
    keep = lax.dynamic_index_in_dim(value, at, 0, keepdims=False)
    send = lax.dynamic_index_in_dim(value, 1 - at, 0, keepdims=False)
    return keep + lax.ppermute(send, axis, [(0, 1), (1, 0)])


def per_device(
    image, upstream, group_ids, group_weights, conv_kernel, norm_gain, first_weight, first_bias, second_weight, layer_scale
):
    core = lax.axis_index("core")
    half = lax.axis_index("xh")
    column = lax.axis_index("z")
    place = jnp.stack([half * 2 + core, column]).astype(jnp.int32)
    one, two = pack_weights(place, first_weight, first_bias, second_weight)
    two = lax.all_gather(two, "z", axis=0, tiled=True).reshape(8, 2 * OWN, CH)
    one = to_all(one, "z")
    one_other = swap_core(one)

    kernel = conv_kernel.reshape(49, CH)
    gain = norm_gain.reshape(1, CH)
    layer = layer_scale.reshape(1, CH)
    normed, centred, inv = forward(image[0], kernel, gain)
    normed_all = ring_share(normed)

    labels = jnp.arange(group_weights.shape[0], dtype=jnp.int32)
    own_weight = jnp.sum(jnp.where(labels == group_ids[0], group_weights, 0.0))
    scaled = (own_weight * upstream[0].astype(F32)).astype(BF16)
    scaled = jnp.pad(scaled, ((0, 0), (0, WIDE - COLS), (0, 0))).reshape(PIX, CH)
    scaled_all = ring_share(scaled)

    act, slope = activations(normed_all, one, one_other)
    preact_grad, *parts = hidden(scaled_all, one, one_other, two, layer, slope)
    grads, other, scale = weight_grads(normed_all, scaled_all, act, preact_grad, two, layer)
    parts[1], parts[2], parts[3], other = lax.optimization_barrier((parts[1], parts[2], parts[3], other))
    got = swap_core(other)
    grads = (grads.astype(F32) + got.astype(F32)).astype(BF16)
    grads = lax.all_to_all(grads, ("y", "z"), 0, 0, tiled=True)
    grads = jnp.sum(grads.astype(F32), axis=0)

    returned = [ring(parts[r], 4 - r) for r in range(1, 4)]
    small, conv_grad = backward(own_weight.reshape(1), parts[0], *returned, centred, inv, gain, scale, image[0])
    small = small.reshape(2, 2, 2, OWN, LANES)
    small = halve(small, "core")
    small = halve(small, "xl")
    small = halve(small, "xh")
    small, grads = lax.optimization_barrier((small, grads))
    small = jnp.sum(to_all(small, "z"), axis=0)
    high = small.astype(BF16)
    low = (small - high.astype(F32)).astype(BF16)
    both = to_all(jnp.concatenate([grads.astype(BF16), high, low], axis=0), "y")
    small = jnp.sum(both[:, 80:128, :].astype(F32) + both[:, 128:176, :].astype(F32), axis=0)
    small = to_all(small, TEAM).reshape(BLOCKS, 64, LANES)
    small = small.transpose(1, 0, 2).reshape(64, CH)

    mine = both[:, 0:80, :]
    across = lax.ppermute(mine, "xh", [(0, 1), (1, 0)])
    mine = jnp.where(half == 0, jnp.stack([mine, across]), jnp.stack([across, mine]))
    other = swap_core(mine)

    images = lax.axis_size(REPLICA) * lax.axis_size(SHARD)
    factor = images / small[51, 0]
    grad_first, grad_second = unpack(factor.reshape(1), core.reshape(1).astype(jnp.int32), mine, other)

    def bias_of(gathered):
        rows = gathered[:, 7, 16:19, :].reshape(2, HALF).astype(F32)
        return lax.dynamic_slice(rows, (0, column * OWN), (2, OWN))

    bias_mine, bias_other = bias_of(mine), bias_of(other)
    bias = jnp.stack([jnp.where(core == 0, bias_mine, bias_other), jnp.where(core == 0, bias_other, bias_mine)], axis=1)
    grad_image = (factor * input_grad(conv_grad, kernel, scaled)).astype(BF16)
    small = factor * small
    return (
        grad_image,
        grad_first,
        factor * bias.reshape(4 * OWN),
        grad_second,
        small[0:49].reshape(7, 7, CH),
        small[49],
        small[50],
    )


def solution(mesh):
    fine = Mesh(mesh.devices.reshape(8, 2, 2, 2, 8), ("y", "xh", "core", "xl", "z"))
    images = P((*REPLICA, *SHARD), None, None, None)
    return jax.shard_map(
        per_device,
        mesh=fine,
        in_specs=(
            images,
            images,
            P((*REPLICA, *SHARD)),
            P(),
            P(),
            P(),
            P(None, SHARD),
            P(SHARD),
            P(SHARD, None),
            P(),
        ),
        out_specs=(images, P(None, SHARD), P(SHARD), P(SHARD, None), P(), P(), P()),
        check_vma=False,
    )
```

```python
import functools

import jax
import jax.numpy as jnp
import numpy as np
from jax import lax
from jax.experimental import pallas as pl
from jax.experimental.pallas import tpu as pltpu
from jax.sharding import Mesh, PartitionSpec as P

F32 = jnp.float32
BF16 = jnp.bfloat16
ROWS = 14
COLS = 14
WIDE = 16
PIX = ROWS * WIDE
CH = 768
LANES = 128
BLOCKS = CH // LANES
OWN = 48
UNITS = 2 * OWN
PACK = 2 * UNITS + 16
REPLICA = ("y", "xh", "core")
SHARD = ("xl", "z")
RING = ("xh", "xl")
TEAM = ("core", "xl", "xh")
INTERPRET = False


def params(limit_mib, **more):
    return pltpu.CompilerParams(vmem_limit_bytes=limit_mib * 1024 * 1024, **more)


def nt(left, right):
    return lax.dot_general(left, right, (((1,), (1,)), ((), ())), preferred_element_type=F32)


def tn(left, right):
    return lax.dot_general(left, right, (((0,), (0,)), ((), ())), preferred_element_type=F32)


def whole():
    return pl.BlockSpec(memory_space=pltpu.VMEM)


def scalars():
    return pl.BlockSpec(memory_space=pltpu.SMEM)


def block(*shape):
    return pl.BlockSpec(shape, lambda i: (0,) * len(shape))


def pack_kernel(place_ref, first_ref, bias_ref, second_ref, out_ref):
    q = place_ref[0]
    column = place_ref[1]
    partner = q + 1 - 2 * lax.rem(q, 2)
    row = lax.broadcasted_iota(jnp.int32, (UNITS, 192), 0)
    lane = lax.broadcasted_iota(jnp.int32, (UNITS, 192), 1)
    wanted = jnp.where(row < OWN, row + q * OWN, row - OWN + partner * OWN)
    pick = (lane == wanted).astype(BF16)
    out_ref[0:UNITS, :] = jnp.dot(pick, first_ref[...], preferred_element_type=F32).astype(BF16)
    out_ref[UNITS : 2 * UNITS, :] = jnp.dot(pick, second_ref[...], preferred_element_type=F32).astype(BF16)
    unit = lax.broadcasted_iota(jnp.int32, (192, CH), 0)
    spot = lax.broadcasted_iota(jnp.int32, (192, CH), 1) - column * UNITS
    wanted = jnp.where(spot < OWN, spot + q * OWN, spot - OWN + partner * OWN)
    put = ((unit == wanted) & (spot >= 0) & (spot < UNITS)).astype(BF16)
    bias = jnp.broadcast_to(bias_ref[...], (16, 192))
    high = bias.astype(BF16)
    low = (bias - high.astype(F32)).astype(BF16)
    bias_row = lax.broadcasted_iota(jnp.int32, (16, 192), 0)
    both = jnp.where(bias_row == 0, high.astype(F32), low.astype(F32)).astype(BF16)
    out_ref[2 * UNITS : PACK, :] = jnp.dot(both, put, preferred_element_type=F32).astype(BF16)


def pack_weights(place, first_weight, first_bias, second_weight):
    return pl.pallas_call(
        pack_kernel,
        grid=(1,),
        out_shape=jax.ShapeDtypeStruct((PACK, CH), BF16),
        in_specs=[scalars(), block(192, CH), block(1, 192), block(192, CH)],
        out_specs=block(PACK, CH),
        compiler_params=params(8),
        interpret=INTERPRET,
        name="pack",
    )(place, first_weight.T, first_bias.reshape(1, 192), second_weight)


def taps_sum(padded_ref, kernel, flip):
    halves = []
    for half in range(2):
        total = jnp.zeros((7, WIDE, LANES), F32)
        for b in range(7):
            moved = padded_ref[half * 7 : half * 7 + 13, b : b + WIDE, :]
            for a in range(7):
                tap = (6 - a) * 7 + (6 - b) if flip else a * 7 + b
                total = total + moved[a : a + 7] * kernel[tap : tap + 1, :].reshape(1, 1, LANES)
        halves.append(total)
    return halves


def column_mask():
    return (lax.broadcasted_iota(jnp.int32, (ROWS, WIDE, LANES), 1) < COLS).astype(F32)


def forward_kernel(image_ref, kernel_ref, gain_ref, normed_ref, centred_ref, inv_ref, padded, conv):
    j = pl.program_id(0)

    @pl.when(j == 0)
    def _():
        padded[...] = jnp.zeros_like(padded)

    padded[3:17, 3:17, :] = image_ref[...].astype(F32)
    halves = taps_sum(padded, kernel_ref[...].astype(F32), False)
    conv[j, 0:7] = halves[0]
    conv[j, 7:14] = halves[1]

    @pl.when(j == BLOCKS - 1)
    def _():
        mask = column_mask()
        total = conv[0]
        for i in range(1, BLOCKS):
            total = total + conv[i]
        mean = jnp.sum(total, axis=-1, keepdims=True) * (1.0 / CH)
        square = jnp.zeros((ROWS, WIDE, LANES), F32)
        for i in range(BLOCKS):
            part = conv[i] - mean
            square = square + part * part
        inv = lax.rsqrt(jnp.sum(square, axis=-1, keepdims=True) * (1.0 / CH) + 1e-06)
        inv_ref[...] = jnp.broadcast_to(inv, (ROWS, WIDE, LANES))
        for i in range(BLOCKS):
            part = (conv[i] - mean) * inv * mask
            centred_ref[i] = part
            lanes = slice(i * LANES, (i + 1) * LANES)
            gain = gain_ref[:, lanes].reshape(1, 1, LANES)
            normed_ref[:, lanes] = (part * gain).reshape(PIX, LANES).astype(BF16)


def forward(image, kernel, gain):
    return pl.pallas_call(
        forward_kernel,
        grid=(BLOCKS,),
        out_shape=(
            jax.ShapeDtypeStruct((PIX, CH), BF16),
            jax.ShapeDtypeStruct((BLOCKS, ROWS, WIDE, LANES), F32),
            jax.ShapeDtypeStruct((ROWS, WIDE, LANES), F32),
        ),
        in_specs=[
            pl.BlockSpec((ROWS, COLS, LANES), lambda j: (0, 0, j)),
            pl.BlockSpec((49, LANES), lambda j: (0, j)),
            pl.BlockSpec((1, CH), lambda j: (0, 0)),
        ],
        out_specs=(
            pl.BlockSpec((PIX, CH), lambda j: (0, 0)),
            pl.BlockSpec((BLOCKS, ROWS, WIDE, LANES), lambda j: (0, 0, 0, 0)),
            pl.BlockSpec((ROWS, WIDE, LANES), lambda j: (0, 0, 0)),
        ),
        scratch_shapes=[
            pltpu.VMEM((20, 24, LANES), F32),
            pltpu.VMEM((BLOCKS, ROWS, WIDE, LANES), F32),
        ],
        compiler_params=params(24),
        interpret=INTERPRET,
        name="conv_norm",
    )(image, kernel, gain)


def hidden_kernel(*refs):
    normed_in = refs[0:4]
    scaled_in = refs[4:8]
    pack_in, layer_ref = refs[8:10]
    parts = refs[10:14]
    outs = refs[14:16]
    scale_ref = refs[16]
    normed, scaled, pack, act, grad, sems = refs[17:23]
    copies = [pltpu.make_async_copy(pack_in, pack, sems.at[8])]
    for i in range(4):
        rows = pl.ds(i * PIX, PIX)
        copies.append(pltpu.make_async_copy(normed_in[i], normed.at[rows], sems.at[i]))
        copies.append(pltpu.make_async_copy(scaled_in[i], scaled.at[rows], sems.at[4 + i]))
    for copy in copies:
        copy.start()
    copies[0].wait()
    first = pack[:, 0:UNITS, :].reshape(CH, CH)
    second = pack[:, UNITS : 2 * UNITS, :].reshape(CH, CH)
    bias = jnp.sum(pack[:, 2 * UNITS : PACK, :].astype(F32), axis=0)
    bias = bias[0:1, :] + bias[1:2, :]
    layer = layer_ref[...]
    for i in range(4):
        rows = slice(i * PIX, (i + 1) * PIX)
        copies[1 + 2 * i].wait()
        copies[2 + 2 * i].wait()
        preact = nt(normed[rows, :], first) + bias
        cumulative = 0.5 * (1.0 + lax.erf(preact * 0.7071067811865476))
        slope = cumulative + preact * jnp.exp(-0.5 * preact * preact) * 0.3989422804014327
        act[rows, :] = (preact * cumulative).astype(BF16)
        branch_grad = (scaled[rows, :].astype(F32) * layer).astype(BF16)
        preact_grad = (nt(branch_grad, second) * slope).astype(BF16)
        grad[rows, :] = preact_grad
        parts[i][...] = jnp.dot(preact_grad, first, preferred_element_type=F32).astype(BF16)
    product = tn(act[...], scaled[...])
    scale_ref[...] = jnp.sum((second.astype(F32) * product).reshape(CH // 8, 8, CH), axis=0)
    spread(outs, (product * layer).astype(BF16), 0)
    spread(outs, tn(grad[...], normed[...]).astype(BF16), 18)
    bias = jnp.dot(jnp.ones((16, 4 * PIX), BF16), grad[...], preferred_element_type=F32)
    row = lax.broadcasted_iota(jnp.int32, (16, LANES), 0)
    empty = jnp.zeros((16, LANES), BF16)
    for half in range(2):
        if half == 1:
            bias = pltpu.roll(bias, CH - OWN, 1)
        rows = jnp.zeros((16, LANES), F32)
        for k in range(BLOCKS):
            rows = jnp.where(row == k, bias[:, k * LANES : (k + 1) * LANES], rows)
        rows = rows.astype(BF16)
        for z in range(8):
            for s in range(36, 40):
                outs[half][(s // 5) * 8 + z, (s % 5) * 16 : (s % 5) * 16 + 16, :] = rows if s == 36 else empty


def spread(outs, matrix, start):
    for half in range(2):
        for z in range(8):
            for j in range(BLOCKS):
                for part in range(3):
                    s = start + j * 3 + part
                    row = z * UNITS + half * OWN + part * 16
                    outs[half][(s // 5) * 8 + z, (s % 5) * 16 : (s % 5) * 16 + 16, :] = matrix[
                        row : row + 16, j * LANES : (j + 1) * LANES
                    ]


def hidden(normed, scaled, pack, layer):
    return pl.pallas_call(
        hidden_kernel,
        grid=(1,),
        out_shape=(jax.ShapeDtypeStruct((PIX, CH), BF16),) * 4
        + (jax.ShapeDtypeStruct((64, 80, LANES), BF16),) * 2
        + (jax.ShapeDtypeStruct((8, CH), F32),),
        in_specs=[pl.BlockSpec(memory_space=pl.ANY)] * 9 + [block(1, CH)],
        out_specs=(block(PIX, CH),) * 4 + (block(64, 80, LANES),) * 2 + (block(8, CH),),
        scratch_shapes=[
            pltpu.VMEM((4 * PIX, CH), BF16),
            pltpu.VMEM((4 * PIX, CH), BF16),
            pltpu.VMEM((8, PACK, CH), BF16),
            pltpu.VMEM((4 * PIX, CH), BF16),
            pltpu.VMEM((4 * PIX, CH), BF16),
            pltpu.SemaphoreType.DMA((9,)),
        ],
        compiler_params=params(40),
        interpret=INTERPRET,
        name="hidden",
    )(*normed, *scaled, pack, layer)


def backward_kernel(
    weight_ref, zero_ref, one_ref, two_ref, three_ref, centred_ref, inv_ref, gain_ref, scale_ref, image_ref,
    sums_ref, conv_ref, padded, conv, parts, gains,
):
    j = pl.program_id(0)

    @pl.when(j == 0)
    def _():
        padded[...] = jnp.zeros_like(padded)
        first = jnp.zeros((ROWS, WIDE, LANES), F32)
        second = jnp.zeros((ROWS, WIDE, LANES), F32)
        for i in range(BLOCKS):
            lanes = slice(i * LANES, (i + 1) * LANES)
            grad = (
                zero_ref[:, lanes].astype(F32)
                + one_ref[:, lanes].astype(F32)
                + two_ref[:, lanes].astype(F32)
                + three_ref[:, lanes].astype(F32)
            ).reshape(ROWS, WIDE, LANES)
            centred = centred_ref[i]
            product = grad * centred
            gains[i] = jnp.sum(jnp.sum(product, axis=0).reshape(2, 8, LANES), axis=0)
            gain = gain_ref[:, lanes].reshape(1, 1, LANES)
            gained = grad * gain
            conv[i] = gained
            first = first + gained
            second = second + product * gain
        mean = jnp.sum(first, axis=-1, keepdims=True) * (1.0 / CH)
        slant = jnp.sum(second, axis=-1, keepdims=True) * (1.0 / CH)
        inv = inv_ref[...] * column_mask()
        for i in range(BLOCKS):
            conv[i] = inv * (conv[i] - mean - centred_ref[i] * slant)

    padded[3:17, 3:17, :] = image_ref[...].astype(F32)
    conv_ref[0] = conv[j]
    for half in range(2):
        signal = conv[j, half * 7 : half * 7 + 7]
        for b in range(7):
            moved = padded[half * 7 : half * 7 + 13, b : b + WIDE, :]
            for a in range(7):
                product = jnp.sum(signal * moved[a : a + 7], axis=0)
                product = product[0:8] + product[8:16]
                if half == 0:
                    parts[a * 7 + b] = product
                else:
                    parts[a * 7 + b] += product
    sums_ref[0] = jnp.zeros((64, LANES), F32)
    sums_ref[0, 0:49, :] = jnp.sum(parts[...], axis=1)
    sums_ref[0, 49:50, :] = jnp.sum(gains[j], axis=0, keepdims=True)
    sums_ref[0, 50:51, :] = jnp.sum(scale_ref[...], axis=0, keepdims=True)
    sums_ref[0, 51:52, :] = jnp.full((1, LANES), weight_ref[0], F32)


def backward(weight, zero, one, two, three, centred, inv, gain, scale, image):
    def fixed(*shape):
        return pl.BlockSpec(shape, lambda j: (0,) * len(shape))

    return pl.pallas_call(
        backward_kernel,
        grid=(BLOCKS,),
        out_shape=(
            jax.ShapeDtypeStruct((BLOCKS, 64, LANES), F32),
            jax.ShapeDtypeStruct((BLOCKS, ROWS, WIDE, LANES), F32),
        ),
        in_specs=[
            scalars(),
            fixed(PIX, CH),
            fixed(PIX, CH),
            fixed(PIX, CH),
            fixed(PIX, CH),
            fixed(BLOCKS, ROWS, WIDE, LANES),
            fixed(ROWS, WIDE, LANES),
            fixed(1, CH),
            pl.BlockSpec((8, LANES), lambda j: (0, j)),
            pl.BlockSpec((ROWS, COLS, LANES), lambda j: (0, 0, j)),
        ],
        out_specs=(
            pl.BlockSpec((1, 64, LANES), lambda j: (j, 0, 0)),
            pl.BlockSpec((1, ROWS, WIDE, LANES), lambda j: (j, 0, 0, 0)),
        ),
        scratch_shapes=[
            pltpu.VMEM((20, 24, LANES), F32),
            pltpu.VMEM((BLOCKS, ROWS, WIDE, LANES), F32),
            pltpu.VMEM((49, 8, LANES), F32),
            pltpu.VMEM((BLOCKS, 8, LANES), F32),
        ],
        compiler_params=params(32),
        interpret=INTERPRET,
        name="norm_back",
    )(weight, zero, one, two, three, centred, inv, gain, scale, image)


def input_kernel(conv_ref, kernel_ref, scaled_ref, out_ref, padded):
    @pl.when(pl.program_id(0) == 0)
    def _():
        padded[...] = jnp.zeros_like(padded)

    padded[3:17, 3 : 3 + WIDE, :] = conv_ref[0]
    halves = taps_sum(padded, kernel_ref[...].astype(F32), True)
    for half in range(2):
        rows = slice(half * 7 * WIDE, (half + 1) * 7 * WIDE)
        scaled = scaled_ref[rows, :].astype(F32).reshape(7, WIDE, LANES)
        out_ref[0, half * 7 : half * 7 + 7] = (scaled + halves[half])[:, 0:COLS, :]


def input_grad(conv, kernel, scaled):
    return pl.pallas_call(
        input_kernel,
        grid=(BLOCKS,),
        out_shape=jax.ShapeDtypeStruct((1, ROWS, COLS, CH), F32),
        in_specs=[
            pl.BlockSpec((1, ROWS, WIDE, LANES), lambda j: (j, 0, 0, 0)),
            pl.BlockSpec((49, LANES), lambda j: (0, j)),
            pl.BlockSpec((PIX, LANES), lambda j: (0, j)),
        ],
        out_specs=pl.BlockSpec((1, ROWS, COLS, LANES), lambda j: (0, 0, 0, j)),
        scratch_shapes=[pltpu.VMEM((20, 24, LANES), F32)],
        compiler_params=params(24),
        interpret=INTERPRET,
        name="input_grad",
    )(conv, kernel, scaled)


def finish_kernel(
    images, place_ref, small_ref, pre_ref, mine_ref, mine_core_ref, across_ref, across_core_ref,
    image_ref, first_ref, second_ref, bias_ref, kernel_ref, gain_ref, scale_ref, gathered,
):
    half, core, column = place_ref[0], place_ref[1], place_ref[2]
    factor = images / small_ref[0, 51:52, :]
    gathered[half * 2 + core] = mine_ref[...]
    gathered[half * 2 + 1 - core] = mine_core_ref[...]
    gathered[(1 - half) * 2 + core] = across_ref[...]
    gathered[(1 - half) * 2 + 1 - core] = across_core_ref[...]
    lane = lax.broadcasted_iota(jnp.int32, (8, CH), 1)
    bias = jnp.zeros((8, CH), F32)
    for q in range(4):
        rows = gathered[q, 7, 16:32, :].astype(F32)
        line = jnp.concatenate([rows[k : k + 1, :] for k in range(BLOCKS)], axis=1)
        line = pltpu.roll(jnp.broadcast_to(line, (8, CH)), lax.rem(CH - column * UNITS + q * OWN, CH), 1)
        bias = jnp.where((lane >= q * OWN) & (lane < (q + 1) * OWN), line, bias)
    bias_ref[...] = bias[0:1, 0:192] * jnp.concatenate([factor, factor[:, 0:64]], axis=1)
    for j in range(BLOCKS):
        lanes = slice(j * LANES, (j + 1) * LANES)
        image_ref[0, :, :, lanes] = (pre_ref[0, :, :, lanes] * factor.reshape(1, 1, LANES)).astype(BF16)
        for a in range(7):
            kernel_ref[a, :, lanes] = small_ref[j, a * 7 : a * 7 + 7, :] * factor
        gain_ref[:, lanes] = small_ref[j, 49:50, :] * factor
        scale_ref[:, lanes] = small_ref[j, 50:51, :] * factor
        for q in range(4):
            for part in range(3):
                rows = slice(q * OWN + part * 16, q * OWN + part * 16 + 16)
                for out_ref, start in ((second_ref, 0), (first_ref, 18)):
                    s = start + j * 3 + part
                    piece = gathered[q, s // 5, (s % 5) * 16 : (s % 5) * 16 + 16, :]
                    out_ref[rows, lanes] = piece.astype(F32) * factor


def finish(images, place, small, pre, mine, mine_core, across, across_core):
    return pl.pallas_call(
        functools.partial(finish_kernel, images),
        grid=(1,),
        out_shape=(
            jax.ShapeDtypeStruct((1, ROWS, COLS, CH), BF16),
            jax.ShapeDtypeStruct((192, CH), F32),
            jax.ShapeDtypeStruct((192, CH), F32),
            jax.ShapeDtypeStruct((1, 192), F32),
            jax.ShapeDtypeStruct((7, 7, CH), F32),
            jax.ShapeDtypeStruct((1, CH), F32),
            jax.ShapeDtypeStruct((1, CH), F32),
        ),
        in_specs=[scalars(), block(BLOCKS, 64, LANES), block(1, ROWS, COLS, CH)]
        + [block(8, 80, LANES)] * 4,
        out_specs=(
            block(1, ROWS, COLS, CH),
            block(192, CH),
            block(192, CH),
            block(1, 192),
            block(7, 7, CH),
            block(1, CH),
            block(1, CH),
        ),
        scratch_shapes=[pltpu.VMEM((4, 8, 80, LANES), BF16)],
        compiler_params=params(24),
        interpret=INTERPRET,
        name="finish",
    )(place, small, pre, mine, mine_core, across, across_core)


def to_all(value, axes):
    count = lax.axis_size(axes)
    return lax.all_to_all(jnp.broadcast_to(value, (count, *value.shape)), axes, 0, 0, tiled=True)


def swap_core(value):
    return lax.ppermute(value, "core", [(0, 1), (1, 0)])


def ring(value, shift):
    return lax.ppermute(value, RING, [(i, (i + shift) % 4) for i in range(4)])


def ring_share(value):
    return [value] + [ring(value, r) for r in range(1, 4)]


def halve(value, axis):
    at = lax.axis_index(axis)
    keep = lax.dynamic_index_in_dim(value, at, 0, keepdims=False)
    send = lax.dynamic_index_in_dim(value, 1 - at, 0, keepdims=False)
    return keep + lax.ppermute(send, axis, [(0, 1), (1, 0)])


def per_device(
    image, upstream, group_ids, group_weights, conv_kernel, norm_gain, first_weight, first_bias, second_weight, layer_scale
):
    core = lax.axis_index("core")
    half = lax.axis_index("xh")
    column = lax.axis_index("z")
    place = jnp.stack([half * 2 + core, column]).astype(jnp.int32)
    packed = pack_weights(place, first_weight, first_bias, second_weight)
    packed = lax.all_gather(packed, "z", axis=0, tiled=True).reshape(8, PACK, CH)

    kernel = conv_kernel.reshape(49, CH)
    gain = norm_gain.reshape(1, CH)
    layer = layer_scale.reshape(1, CH)
    normed, centred, inv = forward(image[0], kernel, gain)
    normed_all = ring_share(normed)

    labels = jnp.arange(group_weights.shape[0], dtype=jnp.int32)
    own_weight = jnp.sum(jnp.where(labels == group_ids[0], group_weights, 0.0))
    scaled = (own_weight * upstream[0].astype(F32)).astype(BF16)
    scaled = jnp.pad(scaled, ((0, 0), (0, WIDE - COLS), (0, 0))).reshape(PIX, CH)
    scaled_all = ring_share(scaled)

    *parts, grads, other, scale = hidden(normed_all, scaled_all, packed, layer)
    got = swap_core(other)
    grads = (grads.astype(F32) + got.astype(F32)).astype(BF16)
    grads = lax.all_to_all(grads, ("y", "z"), 0, 0, tiled=True)
    grads = jnp.sum(grads.astype(F32), axis=0)

    returned = [ring(parts[r], 4 - r) for r in range(1, 4)]
    small, conv_grad = backward(own_weight.reshape(1), parts[0], *returned, centred, inv, gain, scale, image[0])
    small = small.reshape(2, 2, 2, OWN, LANES)
    small = halve(small, "core")
    small = halve(small, "xl")
    small = halve(small, "xh")
    small, grads = lax.optimization_barrier((small, grads))
    small = jnp.sum(to_all(small, "z"), axis=0)
    high = small.astype(BF16)
    low = (small - high.astype(F32)).astype(BF16)
    both = to_all(jnp.concatenate([grads.astype(BF16), high, low], axis=0), "y")
    small = jnp.sum(both[:, 80:128, :].astype(F32) + both[:, 128:176, :].astype(F32), axis=0)
    small = to_all(small, TEAM).reshape(BLOCKS, 64, LANES)

    mine = both[:, 0:80, :]
    across = lax.ppermute(mine, "xh", [(0, 1), (1, 0)])
    pre = input_grad(conv_grad, kernel, scaled)
    images = float(lax.axis_size(REPLICA) * lax.axis_size(SHARD))
    grad_image, grad_first, grad_second, grad_bias, grad_kernel, grad_gain, grad_scale = finish(
        images,
        jnp.stack([half, core, column]).astype(jnp.int32),
        small, pre, mine, swap_core(mine), across, swap_core(across),
    )
    return (
        grad_image,
        grad_first.T,
        grad_bias.reshape(4 * OWN),
        grad_second,
        grad_kernel,
        grad_gain.reshape(CH),
        grad_scale.reshape(CH),
    )


def solution(mesh):
    fine = Mesh(mesh.devices.reshape(8, 2, 2, 2, 8), ("y", "xh", "core", "xl", "z"))
    images = P((*REPLICA, *SHARD), None, None, None)
    return jax.shard_map(
        per_device,
        mesh=fine,
        in_specs=(
            images,
            images,
            P((*REPLICA, *SHARD)),
            P(),
            P(),
            P(),
            P(None, SHARD),
            P(SHARD),
            P(SHARD, None),
            P(),
        ),
        out_specs=(images, P(None, SHARD), P(SHARD), P(SHARD, None), P(), P(), P()),
        check_vma=False,
    )
```

```python
import functools

import jax
import jax.numpy as jnp
import numpy as np
from jax import lax
from jax.experimental import pallas as pl
from jax.experimental.pallas import tpu as pltpu
from jax.sharding import Mesh, PartitionSpec as P

F32 = jnp.float32
BF16 = jnp.bfloat16
ROWS = 14
COLS = 14
WIDE = 16
PIX = ROWS * WIDE
CH = 768
LANES = 128
BLOCKS = CH // LANES
OWN = 48
UNITS = 2 * OWN
PACK = 2 * UNITS + 16
REPLICA = ("y", "xh", "core")
SHARD = ("xl", "z")
RING = ("xh", "xl")
TEAM = ("core", "xl", "xh")
INTERPRET = False
HIDDEN_MIB = 52


def params(limit_mib, **more):
    return pltpu.CompilerParams(vmem_limit_bytes=limit_mib * 1024 * 1024, **more)


def nt(left, right):
    return lax.dot_general(left, right, (((1,), (1,)), ((), ())), preferred_element_type=F32)


def tn(left, right):
    return lax.dot_general(left, right, (((0,), (0,)), ((), ())), preferred_element_type=F32)


def whole():
    return pl.BlockSpec(memory_space=pltpu.VMEM)


def scalars():
    return pl.BlockSpec(memory_space=pltpu.SMEM)


def block(*shape):
    return pl.BlockSpec(shape, lambda i: (0,) * len(shape))


def pack_kernel(place_ref, first_in, bias_in, second_in, out_ref, first_ref, bias_ref, second_ref, sems):
    pairs = ((first_in, first_ref), (second_in, second_ref), (bias_in, bias_ref))
    copies = [pltpu.make_async_copy(source, target, sems.at[i]) for i, (source, target) in enumerate(pairs)]
    for copy in copies:
        copy.start()
    for copy in copies:
        copy.wait()
    q = place_ref[0]
    column = place_ref[1]
    partner = q + 1 - 2 * lax.rem(q, 2)
    row = lax.broadcasted_iota(jnp.int32, (UNITS, 192), 0)
    lane = lax.broadcasted_iota(jnp.int32, (UNITS, 192), 1)
    wanted = jnp.where(row < OWN, row + q * OWN, row - OWN + partner * OWN)
    pick = (lane == wanted).astype(BF16)
    out_ref[0:UNITS, :] = jnp.dot(pick, first_ref[...], preferred_element_type=F32).astype(BF16)
    out_ref[UNITS : 2 * UNITS, :] = jnp.dot(pick, second_ref[...], preferred_element_type=F32).astype(BF16)
    unit = lax.broadcasted_iota(jnp.int32, (192, CH), 0)
    spot = lax.broadcasted_iota(jnp.int32, (192, CH), 1) - column * UNITS
    wanted = jnp.where(spot < OWN, spot + q * OWN, spot - OWN + partner * OWN)
    put = ((unit == wanted) & (spot >= 0) & (spot < UNITS)).astype(BF16)
    bias = jnp.broadcast_to(bias_ref[...], (16, 192))
    high = bias.astype(BF16)
    low = (bias - high.astype(F32)).astype(BF16)
    bias_row = lax.broadcasted_iota(jnp.int32, (16, 192), 0)
    both = jnp.where(bias_row == 0, high.astype(F32), low.astype(F32)).astype(BF16)
    out_ref[2 * UNITS : PACK, :] = jnp.dot(both, put, preferred_element_type=F32).astype(BF16)


def pack_weights(place, first_weight, first_bias, second_weight):
    return pl.pallas_call(
        pack_kernel,
        grid=(1,),
        out_shape=jax.ShapeDtypeStruct((PACK, CH), BF16),
        in_specs=[scalars()] + [pl.BlockSpec(memory_space=pl.ANY)] * 3,
        out_specs=block(PACK, CH),
        scratch_shapes=[
            pltpu.VMEM((192, CH), BF16),
            pltpu.VMEM((1, 192), F32),
            pltpu.VMEM((192, CH), BF16),
            pltpu.SemaphoreType.DMA((3,)),
        ],
        compiler_params=params(58),
        interpret=INTERPRET,
        name="pack",
    )(place, first_weight.T, first_bias.reshape(1, 192), second_weight)


def taps_sum(padded_ref, kernel, flip):
    halves = []
    for half in range(2):
        total = jnp.zeros((7, WIDE, LANES), F32)
        for b in range(7):
            moved = padded_ref[half * 7 : half * 7 + 13, b : b + WIDE, :]
            for a in range(7):
                tap = (6 - a) * 7 + (6 - b) if flip else a * 7 + b
                total = total + moved[a : a + 7] * kernel[tap : tap + 1, :].reshape(1, 1, LANES)
        halves.append(total)
    return halves


def column_mask():
    return (lax.broadcasted_iota(jnp.int32, (ROWS, WIDE, LANES), 1) < COLS).astype(F32)


def forward_kernel(image_ref, kernel_ref, gain_ref, normed_ref, centred_ref, inv_ref, padded, conv):
    j = pl.program_id(0)

    @pl.when(j == 0)
    def _():
        padded[...] = jnp.zeros_like(padded)

    padded[3:17, 3:17, :] = image_ref[...].astype(F32)
    halves = taps_sum(padded, kernel_ref[...].astype(F32), False)
    conv[j, 0:7] = halves[0]
    conv[j, 7:14] = halves[1]

    @pl.when(j == BLOCKS - 1)
    def _():
        mask = column_mask()
        total = conv[0]
        for i in range(1, BLOCKS):
            total = total + conv[i]
        mean = jnp.sum(total, axis=-1, keepdims=True) * (1.0 / CH)
        square = jnp.zeros((ROWS, WIDE, LANES), F32)
        for i in range(BLOCKS):
            part = conv[i] - mean
            square = square + part * part
        inv = lax.rsqrt(jnp.sum(square, axis=-1, keepdims=True) * (1.0 / CH) + 1e-06)
        inv_ref[...] = jnp.broadcast_to(inv, (ROWS, WIDE, LANES))
        for i in range(BLOCKS):
            part = (conv[i] - mean) * inv * mask
            centred_ref[i] = part
            lanes = slice(i * LANES, (i + 1) * LANES)
            gain = gain_ref[:, lanes].reshape(1, 1, LANES)
            normed_ref[:, lanes] = (part * gain).reshape(PIX, LANES).astype(BF16)


def forward(image, kernel, gain):
    return pl.pallas_call(
        forward_kernel,
        grid=(BLOCKS,),
        out_shape=(
            jax.ShapeDtypeStruct((PIX, CH), BF16),
            jax.ShapeDtypeStruct((BLOCKS, ROWS, WIDE, LANES), F32),
            jax.ShapeDtypeStruct((ROWS, WIDE, LANES), F32),
        ),
        in_specs=[
            pl.BlockSpec((ROWS, COLS, LANES), lambda j: (0, 0, j)),
            pl.BlockSpec((49, LANES), lambda j: (0, j)),
            pl.BlockSpec((1, CH), lambda j: (0, 0)),
        ],
        out_specs=(
            pl.BlockSpec((PIX, CH), lambda j: (0, 0)),
            pl.BlockSpec((BLOCKS, ROWS, WIDE, LANES), lambda j: (0, 0, 0, 0)),
            pl.BlockSpec((ROWS, WIDE, LANES), lambda j: (0, 0, 0)),
        ),
        scratch_shapes=[
            pltpu.VMEM((20, 24, LANES), F32),
            pltpu.VMEM((BLOCKS, ROWS, WIDE, LANES), F32),
        ],
        compiler_params=params(8),
        interpret=INTERPRET,
        name="conv_norm",
    )(image, kernel, gain)


def hidden_kernel(*refs):
    normed_in = refs[0:4]
    scaled_in = refs[4:8]
    pack_in, layer_ref = refs[8:10]
    parts = refs[10:14]
    outs = refs[14:16]
    scale_ref = refs[16]
    normed, scaled, pack, act, grad, sems = refs[17:23]
    copies = [pltpu.make_async_copy(pack_in, pack, sems.at[8])]
    for i in range(4):
        rows = pl.ds(i * PIX, PIX)
        copies.append(pltpu.make_async_copy(normed_in[i], normed.at[rows], sems.at[i]))
        copies.append(pltpu.make_async_copy(scaled_in[i], scaled.at[rows], sems.at[4 + i]))
    for copy in copies:
        copy.start()
    copies[0].wait()
    first = pack[:, 0:UNITS, :].reshape(CH, CH)
    second = pack[:, UNITS : 2 * UNITS, :].reshape(CH, CH)
    bias = jnp.sum(pack[:, 2 * UNITS : PACK, :].astype(F32), axis=0)
    bias = bias[0:1, :] + bias[1:2, :]
    layer = layer_ref[...]
    for i in range(4):
        rows = slice(i * PIX, (i + 1) * PIX)
        copies[1 + 2 * i].wait()
        copies[2 + 2 * i].wait()
        preact = nt(normed[rows, :], first) + bias
        cumulative = 0.5 * (1.0 + lax.erf(preact * 0.7071067811865476))
        slope = cumulative + preact * jnp.exp(-0.5 * preact * preact) * 0.3989422804014327
        act[rows, :] = (preact * cumulative).astype(BF16)
        branch_grad = (scaled[rows, :].astype(F32) * layer).astype(BF16)
        preact_grad = (nt(branch_grad, second) * slope).astype(BF16)
        grad[rows, :] = preact_grad
        parts[i][...] = jnp.dot(preact_grad, first, preferred_element_type=F32).astype(BF16)
    product = tn(act[...], scaled[...])
    scale_ref[...] = jnp.sum((second.astype(F32) * product).reshape(CH // 8, 8, CH), axis=0)
    spread(outs, (product * layer).astype(BF16), 0)
    spread(outs, tn(grad[...], normed[...]).astype(BF16), 18)
    bias = jnp.dot(jnp.ones((16, 4 * PIX), BF16), grad[...], preferred_element_type=F32)
    row = lax.broadcasted_iota(jnp.int32, (16, LANES), 0)
    empty = jnp.zeros((16, LANES), BF16)
    for half in range(2):
        if half == 1:
            bias = pltpu.roll(bias, CH - OWN, 1)
        rows = jnp.zeros((16, LANES), F32)
        for k in range(BLOCKS):
            rows = jnp.where(row == k, bias[:, k * LANES : (k + 1) * LANES], rows)
        rows = rows.astype(BF16)
        for z in range(8):
            for s in range(36, 40):
                outs[half][z, s * 16 : s * 16 + 16, :] = rows if s == 36 else empty


def spread(outs, matrix, start):
    for half in range(2):
        for z in range(8):
            for j in range(BLOCKS):
                for part in range(3):
                    s = start + j * 3 + part
                    row = z * UNITS + half * OWN + part * 16
                    outs[half][z, s * 16 : s * 16 + 16, :] = matrix[
                        row : row + 16, j * LANES : (j + 1) * LANES
                    ]


def hidden(normed, scaled, pack, layer):
    return pl.pallas_call(
        hidden_kernel,
        grid=(1,),
        out_shape=(jax.ShapeDtypeStruct((PIX, CH), BF16),) * 4
        + (jax.ShapeDtypeStruct((8, 640, LANES), BF16),) * 2
        + (jax.ShapeDtypeStruct((8, CH), F32),),
        in_specs=[pl.BlockSpec(memory_space=pl.ANY)] * 9 + [block(1, CH)],
        out_specs=(block(PIX, CH),) * 4 + (block(8, 640, LANES),) * 2 + (block(8, CH),),
        scratch_shapes=[
            pltpu.VMEM((4 * PIX, CH), BF16),
            pltpu.VMEM((4 * PIX, CH), BF16),
            pltpu.VMEM((8, PACK, CH), BF16),
            pltpu.VMEM((4 * PIX, CH), BF16),
            pltpu.VMEM((4 * PIX, CH), BF16),
            pltpu.SemaphoreType.DMA((9,)),
        ],
        compiler_params=params(HIDDEN_MIB),
        interpret=INTERPRET,
        name="hidden",
    )(*normed, *scaled, pack, layer)


def backward_kernel(
    weight_ref, zero_ref, one_ref, two_ref, three_ref, centred_ref, inv_ref, gain_ref, scale_ref, image_ref,
    sums_ref, conv_ref, padded, conv, parts, gains,
):
    j = pl.program_id(0)

    @pl.when(j == 0)
    def _():
        padded[...] = jnp.zeros_like(padded)
        first = jnp.zeros((ROWS, WIDE, LANES), F32)
        second = jnp.zeros((ROWS, WIDE, LANES), F32)
        for i in range(BLOCKS):
            lanes = slice(i * LANES, (i + 1) * LANES)
            grad = (
                zero_ref[:, lanes].astype(F32)
                + one_ref[:, lanes].astype(F32)
                + two_ref[:, lanes].astype(F32)
                + three_ref[:, lanes].astype(F32)
            ).reshape(ROWS, WIDE, LANES)
            centred = centred_ref[i]
            product = grad * centred
            gains[i] = jnp.sum(jnp.sum(product, axis=0).reshape(2, 8, LANES), axis=0)
            gain = gain_ref[:, lanes].reshape(1, 1, LANES)
            gained = grad * gain
            conv[i] = gained
            first = first + gained
            second = second + product * gain
        mean = jnp.sum(first, axis=-1, keepdims=True) * (1.0 / CH)
        slant = jnp.sum(second, axis=-1, keepdims=True) * (1.0 / CH)
        inv = inv_ref[...] * column_mask()
        for i in range(BLOCKS):
            conv[i] = inv * (conv[i] - mean - centred_ref[i] * slant)

    padded[3:17, 3:17, :] = image_ref[...].astype(F32)
    conv_ref[0] = conv[j]
    for half in range(2):
        signal = conv[j, half * 7 : half * 7 + 7]
        for b in range(7):
            moved = padded[half * 7 : half * 7 + 13, b : b + WIDE, :]
            for a in range(7):
                product = jnp.sum(signal * moved[a : a + 7], axis=0)
                product = product[0:8] + product[8:16]
                if half == 0:
                    parts[a * 7 + b] = product
                else:
                    parts[a * 7 + b] += product
    sums_ref[0] = jnp.zeros((64, LANES), F32)
    sums_ref[0, 0:49, :] = jnp.sum(parts[...], axis=1)
    sums_ref[0, 49:50, :] = jnp.sum(gains[j], axis=0, keepdims=True)
    sums_ref[0, 50:51, :] = jnp.sum(scale_ref[...], axis=0, keepdims=True)
    sums_ref[0, 51:52, :] = jnp.full((1, LANES), weight_ref[0], F32)


def backward(weight, zero, one, two, three, centred, inv, gain, scale, image):
    def fixed(*shape):
        return pl.BlockSpec(shape, lambda j: (0,) * len(shape))

    return pl.pallas_call(
        backward_kernel,
        grid=(BLOCKS,),
        out_shape=(
            jax.ShapeDtypeStruct((BLOCKS, 64, LANES), F32),
            jax.ShapeDtypeStruct((BLOCKS, ROWS, WIDE, LANES), F32),
        ),
        in_specs=[
            scalars(),
            fixed(PIX, CH),
            fixed(PIX, CH),
            fixed(PIX, CH),
            fixed(PIX, CH),
            fixed(BLOCKS, ROWS, WIDE, LANES),
            fixed(ROWS, WIDE, LANES),
            fixed(1, CH),
            pl.BlockSpec((8, LANES), lambda j: (0, j)),
            pl.BlockSpec((ROWS, COLS, LANES), lambda j: (0, 0, j)),
        ],
        out_specs=(
            pl.BlockSpec((1, 64, LANES), lambda j: (j, 0, 0)),
            pl.BlockSpec((1, ROWS, WIDE, LANES), lambda j: (j, 0, 0, 0)),
        ),
        scratch_shapes=[
            pltpu.VMEM((20, 24, LANES), F32),
            pltpu.VMEM((BLOCKS, ROWS, WIDE, LANES), F32),
            pltpu.VMEM((49, 8, LANES), F32),
            pltpu.VMEM((BLOCKS, 8, LANES), F32),
        ],
        compiler_params=params(12),
        interpret=INTERPRET,
        name="norm_back",
    )(weight, zero, one, two, three, centred, inv, gain, scale, image)


def input_kernel(conv_ref, kernel_ref, scaled_ref, out_ref, padded):
    @pl.when(pl.program_id(0) == 0)
    def _():
        padded[...] = jnp.zeros_like(padded)

    padded[3:17, 3 : 3 + WIDE, :] = conv_ref[0]
    halves = taps_sum(padded, kernel_ref[...].astype(F32), True)
    for half in range(2):
        rows = slice(half * 7 * WIDE, (half + 1) * 7 * WIDE)
        scaled = scaled_ref[rows, :].astype(F32).reshape(7, WIDE, LANES)
        out_ref[0, half * 7 : half * 7 + 7] = (scaled + halves[half])[:, 0:COLS, :]


def input_grad(conv, kernel, scaled):
    return pl.pallas_call(
        input_kernel,
        grid=(BLOCKS,),
        out_shape=jax.ShapeDtypeStruct((1, ROWS, COLS, CH), F32),
        in_specs=[
            pl.BlockSpec((1, ROWS, WIDE, LANES), lambda j: (j, 0, 0, 0)),
            pl.BlockSpec((49, LANES), lambda j: (0, j)),
            pl.BlockSpec((PIX, LANES), lambda j: (0, j)),
        ],
        out_specs=pl.BlockSpec((1, ROWS, COLS, LANES), lambda j: (0, 0, 0, j)),
        scratch_shapes=[pltpu.VMEM((20, 24, LANES), F32)],
        compiler_params=params(6),
        interpret=INTERPRET,
        name="input_grad",
    )(conv, kernel, scaled)


def finish_kernel(
    images, place_ref, small_ref, pre_ref, mine_ref, mine_core_ref, across_ref, across_core_ref,
    image_ref, first_ref, second_ref, bias_ref, kernel_ref, gain_ref, scale_ref, gathered,
):
    half, core, column = place_ref[0], place_ref[1], place_ref[2]
    factor = images / small_ref[0, 51:52, :]
    gathered[half * 2 + core] = mine_ref[...]
    gathered[half * 2 + 1 - core] = mine_core_ref[...]
    gathered[(1 - half) * 2 + core] = across_ref[...]
    gathered[(1 - half) * 2 + 1 - core] = across_core_ref[...]
    lane = lax.broadcasted_iota(jnp.int32, (8, CH), 1)
    bias = jnp.zeros((8, CH), F32)
    for q in range(4):
        rows = gathered[q, 7, 16:32, :].astype(F32)
        line = jnp.concatenate([rows[k : k + 1, :] for k in range(BLOCKS)], axis=1)
        line = pltpu.roll(jnp.broadcast_to(line, (8, CH)), lax.rem(CH - column * UNITS + q * OWN, CH), 1)
        bias = jnp.where((lane >= q * OWN) & (lane < (q + 1) * OWN), line, bias)
    bias_ref[...] = bias[0:1, 0:192] * jnp.concatenate([factor, factor[:, 0:64]], axis=1)
    for j in range(BLOCKS):
        lanes = slice(j * LANES, (j + 1) * LANES)
        image_ref[0, :, :, lanes] = (pre_ref[0, :, :, lanes] * factor.reshape(1, 1, LANES)).astype(BF16)
        for a in range(7):
            kernel_ref[a, :, lanes] = small_ref[j, a * 7 : a * 7 + 7, :] * factor
        gain_ref[lanes] = small_ref[j, 49, :] * factor[0]
        scale_ref[lanes] = small_ref[j, 50, :] * factor[0]
        for q in range(4):
            for part in range(3):
                rows = slice(q * OWN + part * 16, q * OWN + part * 16 + 16)
                for out_ref, start in ((second_ref, 0), (first_ref, 18)):
                    s = start + j * 3 + part
                    piece = gathered[q, s // 5, (s % 5) * 16 : (s % 5) * 16 + 16, :]
                    out_ref[rows, lanes] = piece.astype(F32) * factor


def finish(images, place, small, pre, mine, mine_core, across, across_core):
    return pl.pallas_call(
        functools.partial(finish_kernel, images),
        grid=(1,),
        out_shape=(
            jax.ShapeDtypeStruct((1, ROWS, COLS, CH), BF16),
            jax.ShapeDtypeStruct((192, CH), F32),
            jax.ShapeDtypeStruct((192, CH), F32),
            jax.ShapeDtypeStruct((1, 192), F32),
            jax.ShapeDtypeStruct((7, 7, CH), F32),
            jax.ShapeDtypeStruct((CH,), F32),
            jax.ShapeDtypeStruct((CH,), F32),
        ),
        in_specs=[scalars(), block(BLOCKS, 64, LANES), block(1, ROWS, COLS, CH)]
        + [block(8, 80, LANES)] * 4,
        out_specs=(
            block(1, ROWS, COLS, CH),
            block(192, CH),
            block(192, CH),
            block(1, 192),
            block(7, 7, CH),
            block(CH),
            block(CH),
        ),
        scratch_shapes=[pltpu.VMEM((4, 8, 80, LANES), BF16)],
        compiler_params=params(12),
        interpret=INTERPRET,
        name="finish",
    )(place, small, pre, mine, mine_core, across, across_core)


def to_all(value, axes):
    count = lax.axis_size(axes)
    return lax.all_to_all(jnp.broadcast_to(value, (count, *value.shape)), axes, 0, 0, tiled=True)


def swap_core(value):
    return lax.ppermute(value, "core", [(0, 1), (1, 0)])


def ring(value, shift):
    return lax.ppermute(value, RING, [(i, (i + shift) % 4) for i in range(4)])


def ring_share(value):
    return [value] + [ring(value, r) for r in range(1, 4)]


def per_device(
    image, upstream, group_ids, group_weights, conv_kernel, norm_gain, first_weight, first_bias, second_weight, layer_scale
):
    core = lax.axis_index("core")
    half = lax.axis_index("xh")
    column = lax.axis_index("z")
    place = jnp.stack([half * 2 + core, column]).astype(jnp.int32)
    packed = pack_weights(place, first_weight, first_bias, second_weight)
    packed = lax.all_gather(packed, "z", axis=0, tiled=True).reshape(8, PACK, CH)

    kernel = conv_kernel.reshape(49, CH)
    gain = norm_gain.reshape(1, CH)
    layer = layer_scale.reshape(1, CH)
    normed, centred, inv = forward(image[0], kernel, gain)
    normed_all = ring_share(normed)

    labels = jnp.arange(group_weights.shape[0], dtype=jnp.int32)
    own_weight = jnp.sum(jnp.where(labels == group_ids[0], group_weights, 0.0))
    scaled = (own_weight * upstream[0].astype(F32)).astype(BF16)
    scaled = jnp.pad(scaled, ((0, 0), (0, WIDE - COLS), (0, 0))).reshape(PIX, CH)
    scaled_all = ring_share(scaled)

    *parts, grads, other, scale = hidden(normed_all, scaled_all, packed, layer)
    grads = (grads.astype(F32) + swap_core(other).astype(F32)).astype(BF16)
    grads = lax.psum_scatter(grads, "z", scatter_dimension=0, tiled=True).reshape(8, 80, LANES)

    returned = [ring(parts[r], 4 - r) for r in range(1, 4)]
    small, conv_grad = backward(own_weight.reshape(1), parts[0], *returned, centred, inv, gain, scale, image[0])
    small = lax.all_to_all(small.reshape(8, OWN, LANES), TEAM, 0, 0, tiled=True)
    small = jnp.sum(to_all(jnp.sum(small, axis=0), "z"), axis=0)
    high = small.astype(BF16)
    low = (small - high.astype(F32)).astype(BF16)
    both = jnp.broadcast_to(jnp.concatenate([high, low], axis=0), (8, 2 * OWN, LANES))
    both = lax.all_to_all(jnp.concatenate([grads, both], axis=1), "y", 0, 0, tiled=True).astype(F32)
    mine = to_all(jnp.sum(both[:, 0:80, :], axis=0).astype(BF16), "y")
    small = jnp.sum(both[:, 80:128, :] + both[:, 128:176, :], axis=0)
    small, mine = lax.optimization_barrier((small, mine))
    small = to_all(small, TEAM).reshape(BLOCKS, 64, LANES)

    across = lax.ppermute(mine, "xh", [(0, 1), (1, 0)])
    pre = input_grad(conv_grad, kernel, scaled)
    images = float(lax.axis_size(REPLICA) * lax.axis_size(SHARD))
    grad_image, grad_first, grad_second, grad_bias, grad_kernel, grad_gain, grad_scale = finish(
        images,
        jnp.stack([half, core, column]).astype(jnp.int32),
        small, pre, mine, swap_core(mine), across, swap_core(across),
    )
    return (
        grad_image,
        grad_first.T,
        grad_bias.reshape(4 * OWN),
        grad_second,
        grad_kernel,
        grad_gain,
        grad_scale,
    )


def solution(mesh):
    fine = Mesh(mesh.devices.reshape(8, 2, 2, 2, 8), ("y", "xh", "core", "xl", "z"))
    images = P((*REPLICA, *SHARD), None, None, None)
    return jax.shard_map(
        per_device,
        mesh=fine,
        in_specs=(
            images,
            images,
            P((*REPLICA, *SHARD)),
            P(),
            P(),
            P(),
            P(None, SHARD),
            P(SHARD),
            P(SHARD, None),
            P(),
        ),
        out_specs=(images, P(None, SHARD), P(SHARD), P(SHARD, None), P(), P(), P()),
        check_vma=False,
    )
```

```python
import functools

import jax
import jax.numpy as jnp
import numpy as np
from jax import lax
from jax.experimental import pallas as pl
from jax.experimental.pallas import tpu as pltpu
from jax.sharding import Mesh, PartitionSpec as P

F32 = jnp.float32
BF16 = jnp.bfloat16
ROWS = 14
COLS = 14
WIDE = 16
PIX = ROWS * WIDE
CH = 768
LANES = 128
BLOCKS = CH // LANES
OWN = 48
UNITS = 2 * OWN
PACK = 2 * UNITS + 16
REPLICA = ("y", "xh", "core")
SHARD = ("xl", "z")
RING = ("xh", "xl")
TEAM = ("core", "xl", "xh")
INTERPRET = False
HIDDEN_MIB = 52


def params(limit_mib, **more):
    return pltpu.CompilerParams(vmem_limit_bytes=limit_mib * 1024 * 1024, **more)


def nt(left, right):
    return lax.dot_general(left, right, (((1,), (1,)), ((), ())), preferred_element_type=F32)


def tn(left, right):
    return lax.dot_general(left, right, (((0,), (0,)), ((), ())), preferred_element_type=F32)


def whole():
    return pl.BlockSpec(memory_space=pltpu.VMEM)


def scalars():
    return pl.BlockSpec(memory_space=pltpu.SMEM)


def block(*shape):
    return pl.BlockSpec(shape, lambda i: (0,) * len(shape))


def pack_kernel(place_ref, first_in, bias_in, second_in, out_ref, first_ref, bias_ref, second_ref, sems):
    pairs = ((first_in, first_ref), (second_in, second_ref), (bias_in, bias_ref))
    copies = [pltpu.make_async_copy(source, target, sems.at[i]) for i, (source, target) in enumerate(pairs)]
    for copy in copies:
        copy.start()
    for copy in copies:
        copy.wait()
    q = place_ref[0]
    column = place_ref[1]
    partner = q + 1 - 2 * lax.rem(q, 2)
    row = lax.broadcasted_iota(jnp.int32, (UNITS, 192), 0)
    lane = lax.broadcasted_iota(jnp.int32, (UNITS, 192), 1)
    wanted = jnp.where(row < OWN, row + q * OWN, row - OWN + partner * OWN)
    pick = (lane == wanted).astype(BF16)
    out_ref[0:UNITS, :] = jnp.dot(pick, first_ref[...], preferred_element_type=F32).astype(BF16)
    out_ref[UNITS : 2 * UNITS, :] = jnp.dot(pick, second_ref[...], preferred_element_type=F32).astype(BF16)
    unit = lax.broadcasted_iota(jnp.int32, (192, CH), 0)
    spot = lax.broadcasted_iota(jnp.int32, (192, CH), 1) - column * UNITS
    wanted = jnp.where(spot < OWN, spot + q * OWN, spot - OWN + partner * OWN)
    put = ((unit == wanted) & (spot >= 0) & (spot < UNITS)).astype(BF16)
    bias = jnp.broadcast_to(bias_ref[...], (16, 192))
    high = bias.astype(BF16)
    low = (bias - high.astype(F32)).astype(BF16)
    bias_row = lax.broadcasted_iota(jnp.int32, (16, 192), 0)
    both = jnp.where(bias_row == 0, high.astype(F32), low.astype(F32)).astype(BF16)
    out_ref[2 * UNITS : PACK, :] = jnp.dot(both, put, preferred_element_type=F32).astype(BF16)


def pack_weights(place, first_weight, first_bias, second_weight):
    return pl.pallas_call(
        pack_kernel,
        grid=(1,),
        out_shape=jax.ShapeDtypeStruct((PACK, CH), BF16),
        in_specs=[scalars()] + [pl.BlockSpec(memory_space=pl.ANY)] * 3,
        out_specs=block(PACK, CH),
        scratch_shapes=[
            pltpu.VMEM((192, CH), BF16),
            pltpu.VMEM((1, 192), F32),
            pltpu.VMEM((192, CH), BF16),
            pltpu.SemaphoreType.DMA((3,)),
        ],
        compiler_params=params(58),
        interpret=INTERPRET,
        name="pack",
    )(place, first_weight.T, first_bias.reshape(1, 192), second_weight)


def taps_sum(padded_ref, kernel, flip):
    halves = []
    for half in range(2):
        total = jnp.zeros((7, WIDE, LANES), F32)
        for b in range(7):
            moved = padded_ref[half * 7 : half * 7 + 13, b : b + WIDE, :]
            for a in range(7):
                tap = (6 - a) * 7 + (6 - b) if flip else a * 7 + b
                total = total + moved[a : a + 7] * kernel[tap : tap + 1, :].reshape(1, 1, LANES)
        halves.append(total)
    return halves


def column_mask():
    return (lax.broadcasted_iota(jnp.int32, (ROWS, WIDE, LANES), 1) < COLS).astype(F32)


def forward_kernel(image_ref, kernel_ref, gain_ref, normed_ref, centred_ref, inv_ref, padded, conv):
    j = pl.program_id(0)

    @pl.when(j == 0)
    def _():
        padded[...] = jnp.zeros_like(padded)

    padded[3:17, 3:17, :] = image_ref[...].astype(F32)
    halves = taps_sum(padded, kernel_ref[...].astype(F32), False)
    conv[j, 0:7] = halves[0]
    conv[j, 7:14] = halves[1]

    @pl.when(j == BLOCKS - 1)
    def _():
        mask = column_mask()
        total = conv[0]
        for i in range(1, BLOCKS):
            total = total + conv[i]
        mean = jnp.sum(total, axis=-1, keepdims=True) * (1.0 / CH)
        square = jnp.zeros((ROWS, WIDE, LANES), F32)
        for i in range(BLOCKS):
            part = conv[i] - mean
            square = square + part * part
        inv = lax.rsqrt(jnp.sum(square, axis=-1, keepdims=True) * (1.0 / CH) + 1e-06)
        inv_ref[...] = jnp.broadcast_to(inv, (ROWS, WIDE, LANES))
        for i in range(BLOCKS):
            part = (conv[i] - mean) * inv * mask
            centred_ref[i] = part
            lanes = slice(i * LANES, (i + 1) * LANES)
            gain = gain_ref[:, lanes].reshape(1, 1, LANES)
            normed_ref[:, lanes] = (part * gain).reshape(PIX, LANES).astype(BF16)


def forward(image, kernel, gain):
    return pl.pallas_call(
        forward_kernel,
        grid=(BLOCKS,),
        out_shape=(
            jax.ShapeDtypeStruct((PIX, CH), BF16),
            jax.ShapeDtypeStruct((BLOCKS, ROWS, WIDE, LANES), F32),
            jax.ShapeDtypeStruct((ROWS, WIDE, LANES), F32),
        ),
        in_specs=[
            pl.BlockSpec((ROWS, COLS, LANES), lambda j: (0, 0, j)),
            pl.BlockSpec((49, LANES), lambda j: (0, j)),
            pl.BlockSpec((1, CH), lambda j: (0, 0)),
        ],
        out_specs=(
            pl.BlockSpec((PIX, CH), lambda j: (0, 0)),
            pl.BlockSpec((BLOCKS, ROWS, WIDE, LANES), lambda j: (0, 0, 0, 0)),
            pl.BlockSpec((ROWS, WIDE, LANES), lambda j: (0, 0, 0)),
        ),
        scratch_shapes=[
            pltpu.VMEM((20, 24, LANES), F32),
            pltpu.VMEM((BLOCKS, ROWS, WIDE, LANES), F32),
        ],
        compiler_params=params(8),
        interpret=INTERPRET,
        name="conv_norm",
    )(image, kernel, gain)


def hidden_kernel(*refs):
    normed_in = refs[0:4]
    scaled_in = refs[4:8]
    pack_in, layer_ref = refs[8:10]
    parts = refs[10:14]
    out_ref, scale_ref = refs[14:16]
    normed, scaled, pack, act, grad, sems = refs[16:22]
    copies = [pltpu.make_async_copy(pack_in, pack, sems.at[8])]
    for i in range(4):
        rows = pl.ds(i * PIX, PIX)
        copies.append(pltpu.make_async_copy(normed_in[i], normed.at[rows], sems.at[i]))
        copies.append(pltpu.make_async_copy(scaled_in[i], scaled.at[rows], sems.at[4 + i]))
    for copy in copies:
        copy.start()
    copies[0].wait()
    first = pack[:, 0:UNITS, :].reshape(CH, CH)
    second = pack[:, UNITS : 2 * UNITS, :].reshape(CH, CH)
    bias = jnp.sum(pack[:, 2 * UNITS : PACK, :].astype(F32), axis=0)
    bias = bias[0:1, :] + bias[1:2, :]
    layer = layer_ref[...]
    for i in range(4):
        rows = slice(i * PIX, (i + 1) * PIX)
        copies[1 + 2 * i].wait()
        copies[2 + 2 * i].wait()
        preact = nt(normed[rows, :], first) + bias
        cumulative = 0.5 * (1.0 + lax.erf(preact * 0.7071067811865476))
        slope = cumulative + preact * jnp.exp(-0.5 * preact * preact) * 0.3989422804014327
        act[rows, :] = (preact * cumulative).astype(BF16)
        branch_grad = (scaled[rows, :].astype(F32) * layer).astype(BF16)
        preact_grad = (nt(branch_grad, second) * slope).astype(BF16)
        grad[rows, :] = preact_grad
        parts[i][...] = jnp.dot(preact_grad, first, preferred_element_type=F32).astype(BF16)
    product = tn(act[...], scaled[...])
    scale_ref[...] = jnp.sum((second.astype(F32) * product).reshape(CH // 8, 8, CH), axis=0)
    spread(out_ref, (product * layer).astype(BF16), 0)
    spread(out_ref, tn(grad[...], normed[...]).astype(BF16), 18)
    bias = jnp.dot(jnp.ones((16, 4 * PIX), BF16), grad[...], preferred_element_type=F32)
    row = lax.broadcasted_iota(jnp.int32, (16, LANES), 0)
    empty = jnp.zeros((16, LANES), BF16)
    for half in range(2):
        if half == 1:
            bias = pltpu.roll(bias, CH - OWN, 1)
        rows = jnp.zeros((16, LANES), F32)
        for k in range(BLOCKS):
            rows = jnp.where(row == k, bias[:, k * LANES : (k + 1) * LANES], rows)
        rows = rows.astype(BF16)
        for z in range(8):
            for s in range(36, 40):
                out_ref[z, half * 640 + s * 16 : half * 640 + s * 16 + 16, :] = rows if s == 36 else empty


def spread(out_ref, matrix, start):
    for half in range(2):
        for z in range(8):
            for j in range(BLOCKS):
                for part in range(3):
                    s = start + j * 3 + part
                    row = z * UNITS + half * OWN + part * 16
                    out_ref[z, half * 640 + s * 16 : half * 640 + s * 16 + 16, :] = matrix[
                        row : row + 16, j * LANES : (j + 1) * LANES
                    ]


def hidden(normed, scaled, pack, layer):
    return pl.pallas_call(
        hidden_kernel,
        grid=(1,),
        out_shape=(jax.ShapeDtypeStruct((PIX, CH), BF16),) * 4
        + (jax.ShapeDtypeStruct((8, 1280, LANES), BF16),)
        + (jax.ShapeDtypeStruct((8, CH), F32),),
        in_specs=[pl.BlockSpec(memory_space=pl.ANY)] * 9 + [block(1, CH)],
        out_specs=(block(PIX, CH),) * 4 + (block(8, 1280, LANES),) + (block(8, CH),),
        scratch_shapes=[
            pltpu.VMEM((4 * PIX, CH), BF16),
            pltpu.VMEM((4 * PIX, CH), BF16),
            pltpu.VMEM((8, PACK, CH), BF16),
            pltpu.VMEM((4 * PIX, CH), BF16),
            pltpu.VMEM((4 * PIX, CH), BF16),
            pltpu.SemaphoreType.DMA((9,)),
        ],
        compiler_params=params(HIDDEN_MIB),
        interpret=INTERPRET,
        name="hidden",
    )(*normed, *scaled, pack, layer)


def backward_kernel(
    weight_ref, zero_ref, one_ref, two_ref, three_ref, centred_ref, inv_ref, gain_ref, scale_ref, image_ref,
    sums_ref, conv_ref, padded, conv, parts, gains,
):
    j = pl.program_id(0)

    @pl.when(j == 0)
    def _():
        padded[...] = jnp.zeros_like(padded)
        first = jnp.zeros((ROWS, WIDE, LANES), F32)
        second = jnp.zeros((ROWS, WIDE, LANES), F32)
        for i in range(BLOCKS):
            lanes = slice(i * LANES, (i + 1) * LANES)
            grad = (
                zero_ref[:, lanes].astype(F32)
                + one_ref[:, lanes].astype(F32)
                + two_ref[:, lanes].astype(F32)
                + three_ref[:, lanes].astype(F32)
            ).reshape(ROWS, WIDE, LANES)
            centred = centred_ref[i]
            product = grad * centred
            gains[i] = jnp.sum(jnp.sum(product, axis=0).reshape(2, 8, LANES), axis=0)
            gain = gain_ref[:, lanes].reshape(1, 1, LANES)
            gained = grad * gain
            conv[i] = gained
            first = first + gained
            second = second + product * gain
        mean = jnp.sum(first, axis=-1, keepdims=True) * (1.0 / CH)
        slant = jnp.sum(second, axis=-1, keepdims=True) * (1.0 / CH)
        inv = inv_ref[...] * column_mask()
        for i in range(BLOCKS):
            conv[i] = inv * (conv[i] - mean - centred_ref[i] * slant)

    padded[3:17, 3:17, :] = image_ref[...].astype(F32)
    conv_ref[0] = conv[j]
    for half in range(2):
        signal = conv[j, half * 7 : half * 7 + 7]
        for b in range(7):
            moved = padded[half * 7 : half * 7 + 13, b : b + WIDE, :]
            for a in range(7):
                product = jnp.sum(signal * moved[a : a + 7], axis=0)
                product = product[0:8] + product[8:16]
                if half == 0:
                    parts[a * 7 + b] = product
                else:
                    parts[a * 7 + b] += product
    sums_ref[0] = jnp.zeros((64, LANES), F32)
    sums_ref[0, 0:49, :] = jnp.sum(parts[...], axis=1)
    sums_ref[0, 49:50, :] = jnp.sum(gains[j], axis=0, keepdims=True)
    sums_ref[0, 50:51, :] = jnp.sum(scale_ref[...], axis=0, keepdims=True)
    sums_ref[0, 51:52, :] = jnp.full((1, LANES), weight_ref[0], F32)


def backward(weight, zero, one, two, three, centred, inv, gain, scale, image):
    def fixed(*shape):
        return pl.BlockSpec(shape, lambda j: (0,) * len(shape))

    return pl.pallas_call(
        backward_kernel,
        grid=(BLOCKS,),
        out_shape=(
            jax.ShapeDtypeStruct((BLOCKS, 64, LANES), F32),
            jax.ShapeDtypeStruct((BLOCKS, ROWS, WIDE, LANES), F32),
        ),
        in_specs=[
            scalars(),
            fixed(PIX, CH),
            fixed(PIX, CH),
            fixed(PIX, CH),
            fixed(PIX, CH),
            fixed(BLOCKS, ROWS, WIDE, LANES),
            fixed(ROWS, WIDE, LANES),
            fixed(1, CH),
            pl.BlockSpec((8, LANES), lambda j: (0, j)),
            pl.BlockSpec((ROWS, COLS, LANES), lambda j: (0, 0, j)),
        ],
        out_specs=(
            pl.BlockSpec((1, 64, LANES), lambda j: (j, 0, 0)),
            pl.BlockSpec((1, ROWS, WIDE, LANES), lambda j: (j, 0, 0, 0)),
        ),
        scratch_shapes=[
            pltpu.VMEM((20, 24, LANES), F32),
            pltpu.VMEM((BLOCKS, ROWS, WIDE, LANES), F32),
            pltpu.VMEM((49, 8, LANES), F32),
            pltpu.VMEM((BLOCKS, 8, LANES), F32),
        ],
        compiler_params=params(12),
        interpret=INTERPRET,
        name="norm_back",
    )(weight, zero, one, two, three, centred, inv, gain, scale, image)


def input_kernel(conv_ref, kernel_ref, scaled_ref, out_ref, padded):
    @pl.when(pl.program_id(0) == 0)
    def _():
        padded[...] = jnp.zeros_like(padded)

    padded[3:17, 3 : 3 + WIDE, :] = conv_ref[0]
    halves = taps_sum(padded, kernel_ref[...].astype(F32), True)
    for half in range(2):
        rows = slice(half * 7 * WIDE, (half + 1) * 7 * WIDE)
        scaled = scaled_ref[rows, :].astype(F32).reshape(7, WIDE, LANES)
        out_ref[0, half * 7 : half * 7 + 7] = (scaled + halves[half])[:, 0:COLS, :]


def input_grad(conv, kernel, scaled):
    return pl.pallas_call(
        input_kernel,
        grid=(BLOCKS,),
        out_shape=jax.ShapeDtypeStruct((1, ROWS, COLS, CH), F32),
        in_specs=[
            pl.BlockSpec((1, ROWS, WIDE, LANES), lambda j: (j, 0, 0, 0)),
            pl.BlockSpec((49, LANES), lambda j: (0, j)),
            pl.BlockSpec((PIX, LANES), lambda j: (0, j)),
        ],
        out_specs=pl.BlockSpec((1, ROWS, COLS, LANES), lambda j: (0, 0, 0, j)),
        scratch_shapes=[pltpu.VMEM((20, 24, LANES), F32)],
        compiler_params=params(6),
        interpret=INTERPRET,
        name="input_grad",
    )(conv, kernel, scaled)


def finish_kernel(
    images, place_ref, small_in, small_core_in, pre_ref, mine_ref, other_ref,
    image_ref, first_ref, second_ref, bias_ref, kernel_ref, gain_ref, scale_ref, gathered, small_ref,
):
    half, core, column, pair = place_ref[0], place_ref[1], place_ref[2], place_ref[3]
    for b in range(2):
        gathered[b * 2 + core] = mine_ref[:, b]
        gathered[b * 2 + 1 - core] = other_ref[:, b]
    for a in range(2):
        for b in range(2):
            part = 2 * (pair + a - 2 * a * pair) + (half + b - 2 * b * half)
            rows = slice((a * 2 + b) * OWN, (a * 2 + b + 1) * OWN)
            for first, source in ((core, small_in), (1 - core, small_core_in)):
                small_ref[pl.ds(pl.multiple_of((first * 4 + part) * OWN, OWN), OWN), :] = source[rows, :]
    factor = images / small_ref[51:52, :]
    lane = lax.broadcasted_iota(jnp.int32, (8, CH), 1)
    bias = jnp.zeros((8, CH), F32)
    for q in range(4):
        rows = gathered[q, 7, 16:32, :].astype(F32)
        line = jnp.concatenate([rows[k : k + 1, :] for k in range(BLOCKS)], axis=1)
        line = pltpu.roll(jnp.broadcast_to(line, (8, CH)), lax.rem(CH - column * UNITS + q * OWN, CH), 1)
        bias = jnp.where((lane >= q * OWN) & (lane < (q + 1) * OWN), line, bias)
    bias_ref[...] = bias[0:1, 0:192] * jnp.concatenate([factor, factor[:, 0:64]], axis=1)
    for j in range(BLOCKS):
        lanes = slice(j * LANES, (j + 1) * LANES)
        image_ref[0, :, :, lanes] = (pre_ref[0, :, :, lanes] * factor.reshape(1, 1, LANES)).astype(BF16)
        for a in range(7):
            kernel_ref[a, :, lanes] = small_ref[j * 64 + a * 7 : j * 64 + a * 7 + 7, :] * factor
        gain_ref[lanes] = small_ref[j * 64 + 49, :] * factor[0]
        scale_ref[lanes] = small_ref[j * 64 + 50, :] * factor[0]
        for q in range(4):
            for part in range(3):
                rows = slice(q * OWN + part * 16, q * OWN + part * 16 + 16)
                for out_ref, start in ((second_ref, 0), (first_ref, 18)):
                    s = start + j * 3 + part
                    piece = gathered[q, s // 5, (s % 5) * 16 : (s % 5) * 16 + 16, :]
                    out_ref[rows, lanes] = piece.astype(F32) * factor


def finish(images, place, small, small_core, pre, mine, other):
    return pl.pallas_call(
        functools.partial(finish_kernel, images),
        grid=(1,),
        out_shape=(
            jax.ShapeDtypeStruct((1, ROWS, COLS, CH), BF16),
            jax.ShapeDtypeStruct((192, CH), F32),
            jax.ShapeDtypeStruct((192, CH), F32),
            jax.ShapeDtypeStruct((1, 192), F32),
            jax.ShapeDtypeStruct((7, 7, CH), F32),
            jax.ShapeDtypeStruct((CH,), F32),
            jax.ShapeDtypeStruct((CH,), F32),
        ),
        in_specs=[scalars(), block(4 * OWN, LANES), block(4 * OWN, LANES), block(1, ROWS, COLS, CH)]
        + [block(8, 2, 80, LANES)] * 2,
        out_specs=(
            block(1, ROWS, COLS, CH),
            block(192, CH),
            block(192, CH),
            block(1, 192),
            block(7, 7, CH),
            block(CH),
            block(CH),
        ),
        scratch_shapes=[pltpu.VMEM((4, 8, 80, LANES), BF16), pltpu.VMEM((8 * OWN, LANES), F32)],
        compiler_params=params(12),
        interpret=INTERPRET,
        name="finish",
    )(place, small, small_core, pre, mine, other)


def to_all(value, axes):
    count = lax.axis_size(axes)
    return lax.all_to_all(jnp.broadcast_to(value, (count, *value.shape)), axes, 0, 0, tiled=True)


def swap(axis, value):
    return lax.ppermute(value, axis, [(0, 1), (1, 0)])


def swap_core(value):
    return swap("core", value)


def split(small, holds):
    row = lax.broadcasted_iota(jnp.int32, small.shape, 0)
    rest = small - small.astype(BF16).astype(F32)
    return jnp.where((row == 4) & holds, jnp.roll(rest, 1, 0), small).astype(BF16)


def join(small, holds):
    row = lax.broadcasted_iota(jnp.int32, small.shape, 0)
    return jnp.where((row == 3) & holds, small + jnp.roll(small, -1, 0), small)


def ring(value, shift):
    return lax.ppermute(value, RING, [(i, (i + shift) % 4) for i in range(4)])


def ring_share(value):
    return [value] + [ring(value, r) for r in range(1, 4)]


def per_device(
    image, upstream, group_ids, group_weights, conv_kernel, norm_gain, first_weight, first_bias, second_weight, layer_scale
):
    core = lax.axis_index("core")
    half = lax.axis_index("xh")
    column = lax.axis_index("z")
    place = jnp.stack([half * 2 + core, column]).astype(jnp.int32)
    packed = pack_weights(place, first_weight, first_bias, second_weight)
    packed = lax.all_gather(packed, "z", axis=0, tiled=True).reshape(8, PACK, CH)

    kernel = conv_kernel.reshape(49, CH)
    gain = norm_gain.reshape(1, CH)
    layer = layer_scale.reshape(1, CH)
    normed, centred, inv = forward(image[0], kernel, gain)
    normed_all = ring_share(normed)

    labels = jnp.arange(group_weights.shape[0], dtype=jnp.int32)
    own_weight = jnp.sum(jnp.where(labels == group_ids[0], group_weights, 0.0))
    scaled = (own_weight * upstream[0].astype(F32)).astype(BF16)
    scaled = jnp.pad(scaled, ((0, 0), (0, WIDE - COLS), (0, 0))).reshape(PIX, CH)
    scaled_all = ring_share(scaled)

    *parts, grads, scale = hidden(normed_all, scaled_all, packed, layer)
    grads = lax.psum_scatter(grads, "z", scatter_dimension=0, tiled=True).reshape(2, 8, 80, LANES)
    grads = (grads[0].astype(F32) + swap_core(grads[1]).astype(F32)).astype(BF16)

    returned = [ring(parts[r], 4 - r) for r in range(1, 4)]
    small, conv_grad = backward(own_weight.reshape(1), parts[0], *returned, centred, inv, gain, scale, image[0])
    small = lax.all_to_all(small.reshape(8, OWN, LANES), TEAM, 0, 0, tiled=True)
    holds = lax.axis_index(TEAM) == 1
    small = join(jnp.sum(to_all(split(jnp.sum(small, axis=0), holds), "z").astype(F32), axis=0), holds)
    both = jnp.broadcast_to(split(small, holds), (8, OWN, LANES))
    both = lax.all_to_all(jnp.concatenate([grads, both], axis=1), "y", 0, 0, tiled=True).astype(F32)
    mine = to_all(jnp.sum(both[:, 0:80, :], axis=0).astype(BF16), ("y", "xh")).reshape(8, 2, 80, LANES)
    small = join(jnp.sum(both[:, 80:128, :], axis=0), holds)
    small = jnp.concatenate([small, swap("xh", small)], axis=0)
    small = jnp.concatenate([small, swap("xl", small)], axis=0)
    small, mine = lax.optimization_barrier((small, mine))
    pre = input_grad(conv_grad, kernel, scaled)
    images = float(lax.axis_size(REPLICA) * lax.axis_size(SHARD))
    grad_image, grad_first, grad_second, grad_bias, grad_kernel, grad_gain, grad_scale = finish(
        images,
        jnp.stack([half, core, column, lax.axis_index("xl")]).astype(jnp.int32),
        small, swap_core(small), pre, mine, swap_core(mine),
    )
    return (
        grad_image,
        grad_first.T,
        grad_bias.reshape(4 * OWN),
        grad_second,
        grad_kernel,
        grad_gain,
        grad_scale,
    )


def solution(mesh):
    fine = Mesh(mesh.devices.reshape(8, 2, 2, 2, 8), ("y", "xh", "core", "xl", "z"))
    images = P((*REPLICA, *SHARD), None, None, None)
    return jax.shard_map(
        per_device,
        mesh=fine,
        in_specs=(
            images,
            images,
            P((*REPLICA, *SHARD)),
            P(),
            P(),
            P(),
            P(None, SHARD),
            P(SHARD),
            P(SHARD, None),
            P(),
        ),
        out_specs=(images, P(None, SHARD), P(SHARD), P(SHARD, None), P(), P(), P()),
        check_vma=False,
    )
```

```python
import functools

import jax
import jax.numpy as jnp
import numpy as np
from jax import lax
from jax.experimental import pallas as pl
from jax.experimental.pallas import tpu as pltpu
from jax.sharding import Mesh, PartitionSpec as P

F32 = jnp.float32
BF16 = jnp.bfloat16
ROWS = 14
COLS = 14
WIDE = 16
PIX = ROWS * WIDE
CH = 768
LANES = 128
BLOCKS = CH // LANES
OWN = 48
UNITS = 2 * OWN
PACK = UNITS + 16
REPLICA = ("y", "xh", "core")
SHARD = ("xl", "z")
RING = ("xh", "xl")
TEAM = ("core", "xl", "xh")
INTERPRET = False
HIDDEN_MIB = 52


def params(limit_mib, **more):
    return pltpu.CompilerParams(vmem_limit_bytes=limit_mib * 1024 * 1024, **more)


def nt(left, right):
    return lax.dot_general(left, right, (((1,), (1,)), ((), ())), preferred_element_type=F32)


def tn(left, right):
    return lax.dot_general(left, right, (((0,), (0,)), ((), ())), preferred_element_type=F32)


def whole():
    return pl.BlockSpec(memory_space=pltpu.VMEM)


def scalars():
    return pl.BlockSpec(memory_space=pltpu.SMEM)


def block(*shape):
    return pl.BlockSpec(shape, lambda i: (0,) * len(shape))


def pack_kernel(place_ref, first_in, bias_in, second_in, out_ref, first_ref, bias_ref, second_ref, sems):
    pairs = ((first_in, first_ref), (second_in, second_ref), (bias_in, bias_ref))
    copies = [pltpu.make_async_copy(source, target, sems.at[i]) for i, (source, target) in enumerate(pairs)]
    for copy in copies:
        copy.start()
    for copy in copies:
        copy.wait()
    q = place_ref[0]
    column = place_ref[1]
    for k in range(2):
        at = q + k * (1 - 2 * lax.rem(q, 2))
        row = lax.broadcasted_iota(jnp.int32, (OWN, 192), 0)
        lane = lax.broadcasted_iota(jnp.int32, (OWN, 192), 1)
        pick = (lane == row + at * OWN).astype(BF16)
        out_ref[k, 0:OWN, :] = jnp.dot(pick, first_ref[...], preferred_element_type=F32).astype(BF16)
        out_ref[k, OWN:UNITS, :] = jnp.dot(pick, second_ref[...], preferred_element_type=F32).astype(BF16)
        unit = lax.broadcasted_iota(jnp.int32, (192, CH), 0)
        spot = lax.broadcasted_iota(jnp.int32, (192, CH), 1) - column * UNITS
        put = ((unit == spot + at * OWN) & (spot >= 0) & (spot < OWN)).astype(BF16)
        bias = jnp.broadcast_to(bias_ref[...], (16, 192))
        high = bias.astype(BF16)
        low = (bias - high.astype(F32)).astype(BF16)
        bias_row = lax.broadcasted_iota(jnp.int32, (16, 192), 0)
        both = jnp.where(bias_row == 0, high.astype(F32), low.astype(F32)).astype(BF16)
        out_ref[k, UNITS:PACK, :] = jnp.dot(both, put, preferred_element_type=F32).astype(BF16)


def pack_weights(place, first_weight, first_bias, second_weight):
    return pl.pallas_call(
        pack_kernel,
        grid=(1,),
        out_shape=jax.ShapeDtypeStruct((2, PACK, CH), BF16),
        in_specs=[scalars()] + [pl.BlockSpec(memory_space=pl.ANY)] * 3,
        out_specs=block(2, PACK, CH),
        scratch_shapes=[
            pltpu.VMEM((192, CH), BF16),
            pltpu.VMEM((1, 192), F32),
            pltpu.VMEM((192, CH), BF16),
            pltpu.SemaphoreType.DMA((3,)),
        ],
        compiler_params=params(58),
        interpret=INTERPRET,
        name="pack",
    )(place, first_weight.T, first_bias.reshape(1, 192), second_weight)


def taps_sum(padded_ref, kernel, flip):
    halves = []
    for half in range(2):
        total = jnp.zeros((7, WIDE, LANES), F32)
        for b in range(7):
            moved = padded_ref[half * 7 : half * 7 + 13, b : b + WIDE, :]
            for a in range(7):
                tap = (6 - a) * 7 + (6 - b) if flip else a * 7 + b
                total = total + moved[a : a + 7] * kernel[tap : tap + 1, :].reshape(1, 1, LANES)
        halves.append(total)
    return halves


def column_mask():
    return (lax.broadcasted_iota(jnp.int32, (ROWS, WIDE, LANES), 1) < COLS).astype(F32)


def forward_kernel(image_ref, kernel_ref, gain_ref, normed_ref, centred_ref, inv_ref, padded, conv):
    j = pl.program_id(0)

    @pl.when(j == 0)
    def _():
        padded[...] = jnp.zeros_like(padded)

    padded[3:17, 3:17, :] = image_ref[...].astype(F32)
    halves = taps_sum(padded, kernel_ref[...].astype(F32), False)
    conv[j, 0:7] = halves[0]
    conv[j, 7:14] = halves[1]

    @pl.when(j == BLOCKS - 1)
    def _():
        mask = column_mask()
        total = conv[0]
        for i in range(1, BLOCKS):
            total = total + conv[i]
        mean = jnp.sum(total, axis=-1, keepdims=True) * (1.0 / CH)
        square = jnp.zeros((ROWS, WIDE, LANES), F32)
        for i in range(BLOCKS):
            part = conv[i] - mean
            square = square + part * part
        inv = lax.rsqrt(jnp.sum(square, axis=-1, keepdims=True) * (1.0 / CH) + 1e-06)
        inv_ref[...] = jnp.broadcast_to(inv, (ROWS, WIDE, LANES))
        for i in range(BLOCKS):
            part = (conv[i] - mean) * inv * mask
            centred_ref[i] = part
            lanes = slice(i * LANES, (i + 1) * LANES)
            gain = gain_ref[:, lanes].reshape(1, 1, LANES)
            normed_ref[:, lanes] = (part * gain).reshape(PIX, LANES).astype(BF16)


def forward(image, kernel, gain):
    return pl.pallas_call(
        forward_kernel,
        grid=(BLOCKS,),
        out_shape=(
            jax.ShapeDtypeStruct((PIX, CH), BF16),
            jax.ShapeDtypeStruct((BLOCKS, ROWS, WIDE, LANES), F32),
            jax.ShapeDtypeStruct((ROWS, WIDE, LANES), F32),
        ),
        in_specs=[
            pl.BlockSpec((ROWS, COLS, LANES), lambda j: (0, 0, j)),
            pl.BlockSpec((49, LANES), lambda j: (0, j)),
            pl.BlockSpec((1, CH), lambda j: (0, 0)),
        ],
        out_specs=(
            pl.BlockSpec((PIX, CH), lambda j: (0, 0)),
            pl.BlockSpec((BLOCKS, ROWS, WIDE, LANES), lambda j: (0, 0, 0, 0)),
            pl.BlockSpec((ROWS, WIDE, LANES), lambda j: (0, 0, 0)),
        ),
        scratch_shapes=[
            pltpu.VMEM((20, 24, LANES), F32),
            pltpu.VMEM((BLOCKS, ROWS, WIDE, LANES), F32),
        ],
        compiler_params=params(8),
        interpret=INTERPRET,
        name="conv_norm",
    )(image, kernel, gain)


def hidden_kernel(*refs):
    normed_in = refs[0:4]
    scaled_in = refs[4:8]
    pack_in, layer_ref = refs[8:10]
    part_outs = refs[10:14]
    grads_out, scale_ref = refs[14:16]
    normed, scaled, firsts, seconds, biases, act, grad, parts, out_ref, sems, out_sems = refs[16:27]
    first_copies, second_copies, normed_copies, scaled_copies, sends = [], [], [], [], []
    for k in range(2):
        whole_z = pl.ds(0, 8)
        first_copies.append(
            pltpu.make_async_copy(pack_in.at[whole_z, k, pl.ds(0, OWN)], firsts.at[whole_z, k], sems.at[k])
        )
        first_copies.append(
            pltpu.make_async_copy(pack_in.at[whole_z, k, pl.ds(UNITS, 16)], biases.at[k], sems.at[2 + k])
        )
        second_copies.append(
            pltpu.make_async_copy(pack_in.at[whole_z, k, pl.ds(OWN, OWN)], seconds.at[whole_z, k], sems.at[4 + k])
        )
    for i in range(4):
        rows = pl.ds(i * PIX, PIX)
        normed_copies.append(pltpu.make_async_copy(normed_in[i], normed.at[rows], sems.at[6 + i]))
        scaled_copies.append(pltpu.make_async_copy(scaled_in[i], scaled.at[rows], sems.at[10 + i]))
    for copy in [*first_copies, *normed_copies, *second_copies, *scaled_copies]:
        copy.start()
    for copy in first_copies:
        copy.wait()
    first = firsts[...].reshape(CH, CH)
    halves = []
    for k in range(2):
        rows = jnp.sum(biases[k].astype(F32), axis=0)
        halves.append(jnp.broadcast_to(rows[0:1, :] + rows[1:2, :], (8, CH)))
    bias = (halves[0] + pltpu.roll(halves[1], OWN, 1))[0:1, :]
    layer = layer_ref[...]
    for i in range(4):
        rows = slice(i * PIX, (i + 1) * PIX)
        normed_copies[i].wait()
        preact = nt(normed[rows, :], first) + bias
        cumulative = 0.5 * (1.0 + lax.erf(preact * 0.7071067811865476))
        slope = cumulative + preact * jnp.exp(-0.5 * preact * preact) * 0.3989422804014327
        act[rows, :] = (preact * cumulative).astype(BF16)
        if i == 0:
            for copy in second_copies:
                copy.wait()
            second = seconds[...].reshape(CH, CH)
        scaled_copies[i].wait()
        branch_grad = (scaled[rows, :].astype(F32) * layer).astype(BF16)
        preact_grad = (nt(branch_grad, second) * slope).astype(BF16)
        grad[rows, :] = preact_grad
        parts[rows, :] = jnp.dot(preact_grad, first, preferred_element_type=F32).astype(BF16)
        sends.append(pltpu.make_async_copy(parts.at[pl.ds(i * PIX, PIX)], part_outs[i], out_sems.at[i]))
        sends[-1].start()
    product = tn(act[...], scaled[...])
    scale_ref[...] = jnp.sum((second.astype(F32) * product).reshape(CH // 8, 8, CH), axis=0)
    spread(out_ref, (product * layer).astype(BF16), 0)
    for half in range(2):
        rows = pl.ds(half * 640, 288)
        sends.append(
            pltpu.make_async_copy(
                out_ref.at[pl.ds(0, 8), rows], grads_out.at[pl.ds(0, 8), rows], out_sems.at[4 + half]
            )
        )
        sends[-1].start()
    spread(out_ref, tn(grad[...], normed[...]).astype(BF16), 18)
    bias = jnp.dot(jnp.ones((16, 4 * PIX), BF16), grad[...], preferred_element_type=F32)
    row = lax.broadcasted_iota(jnp.int32, (16, LANES), 0)
    empty = jnp.zeros((16, LANES), BF16)
    for half in range(2):
        if half == 1:
            bias = pltpu.roll(bias, CH - OWN, 1)
        rows = jnp.zeros((16, LANES), F32)
        for k in range(BLOCKS):
            rows = jnp.where(row == k, bias[:, k * LANES : (k + 1) * LANES], rows)
        rows = rows.astype(BF16)
        for z in range(8):
            for s in range(36, 40):
                out_ref[z, half * 640 + s * 16 : half * 640 + s * 16 + 16, :] = rows if s == 36 else empty
        span = pl.ds(half * 640 + 288, 352)
        sends.append(
            pltpu.make_async_copy(
                out_ref.at[pl.ds(0, 8), span], grads_out.at[pl.ds(0, 8), span], out_sems.at[6 + half]
            )
        )
        sends[-1].start()
    for send in sends:
        send.wait()


def spread(out_ref, matrix, start):
    for half in range(2):
        for z in range(8):
            for j in range(BLOCKS):
                for part in range(3):
                    s = start + j * 3 + part
                    row = z * UNITS + half * OWN + part * 16
                    out_ref[z, half * 640 + s * 16 : half * 640 + s * 16 + 16, :] = matrix[
                        row : row + 16, j * LANES : (j + 1) * LANES
                    ]


def hidden(normed, scaled, pack, layer):
    free = pl.BlockSpec(memory_space=pl.ANY)
    return pl.pallas_call(
        hidden_kernel,
        grid=(1,),
        out_shape=(jax.ShapeDtypeStruct((PIX, CH), BF16),) * 4
        + (jax.ShapeDtypeStruct((8, 1280, LANES), BF16),)
        + (jax.ShapeDtypeStruct((8, CH), F32),),
        in_specs=[free] * 9 + [block(1, CH)],
        out_specs=(free,) * 5 + (block(8, CH),),
        scratch_shapes=[
            pltpu.VMEM((4 * PIX, CH), BF16),
            pltpu.VMEM((4 * PIX, CH), BF16),
            pltpu.VMEM((8, 2, OWN, CH), BF16),
            pltpu.VMEM((8, 2, OWN, CH), BF16),
            pltpu.VMEM((2, 8, 16, CH), BF16),
            pltpu.VMEM((4 * PIX, CH), BF16),
            pltpu.VMEM((4 * PIX, CH), BF16),
            pltpu.VMEM((4 * PIX, CH), BF16),
            pltpu.VMEM((8, 1280, LANES), BF16),
            pltpu.SemaphoreType.DMA((14,)),
            pltpu.SemaphoreType.DMA((8,)),
        ],
        compiler_params=params(HIDDEN_MIB),
        interpret=INTERPRET,
        name="hidden",
    )(*normed, *scaled, pack, layer)


def backward_kernel(
    weight_ref, zero_ref, one_ref, two_ref, three_ref, centred_ref, inv_ref, gain_ref, scale_ref, image_ref,
    sums_ref, conv_ref, padded, conv, parts, gains,
):
    j = pl.program_id(0)

    @pl.when(j == 0)
    def _():
        padded[...] = jnp.zeros_like(padded)
        first = jnp.zeros((ROWS, WIDE, LANES), F32)
        second = jnp.zeros((ROWS, WIDE, LANES), F32)
        for i in range(BLOCKS):
            lanes = slice(i * LANES, (i + 1) * LANES)
            grad = (
                zero_ref[:, lanes].astype(F32)
                + one_ref[:, lanes].astype(F32)
                + two_ref[:, lanes].astype(F32)
                + three_ref[:, lanes].astype(F32)
            ).reshape(ROWS, WIDE, LANES)
            centred = centred_ref[i]
            product = grad * centred
            gains[i] = jnp.sum(jnp.sum(product, axis=0).reshape(2, 8, LANES), axis=0)
            gain = gain_ref[:, lanes].reshape(1, 1, LANES)
            gained = grad * gain
            conv[i] = gained
            first = first + gained
            second = second + product * gain
        mean = jnp.sum(first, axis=-1, keepdims=True) * (1.0 / CH)
        slant = jnp.sum(second, axis=-1, keepdims=True) * (1.0 / CH)
        inv = inv_ref[...] * column_mask()
        for i in range(BLOCKS):
            conv[i] = inv * (conv[i] - mean - centred_ref[i] * slant)

    padded[3:17, 3:17, :] = image_ref[...].astype(F32)
    conv_ref[0] = conv[j]
    for half in range(2):
        signal = conv[j, half * 7 : half * 7 + 7]
        for b in range(7):
            moved = padded[half * 7 : half * 7 + 13, b : b + WIDE, :]
            for a in range(7):
                product = jnp.sum(signal * moved[a : a + 7], axis=0)
                product = product[0:8] + product[8:16]
                if half == 0:
                    parts[a * 7 + b] = product
                else:
                    parts[a * 7 + b] += product
    sums_ref[0] = jnp.zeros((64, LANES), F32)
    sums_ref[0, 0:49, :] = jnp.sum(parts[...], axis=1)
    sums_ref[0, 49:50, :] = jnp.sum(gains[j], axis=0, keepdims=True)
    sums_ref[0, 50:51, :] = jnp.sum(scale_ref[...], axis=0, keepdims=True)
    sums_ref[0, 51:52, :] = jnp.full((1, LANES), weight_ref[0], F32)


def backward(weight, zero, one, two, three, centred, inv, gain, scale, image):
    def fixed(*shape):
        return pl.BlockSpec(shape, lambda j: (0,) * len(shape))

    return pl.pallas_call(
        backward_kernel,
        grid=(BLOCKS,),
        out_shape=(
            jax.ShapeDtypeStruct((BLOCKS, 64, LANES), F32),
            jax.ShapeDtypeStruct((BLOCKS, ROWS, WIDE, LANES), F32),
        ),
        in_specs=[
            scalars(),
            fixed(PIX, CH),
            fixed(PIX, CH),
            fixed(PIX, CH),
            fixed(PIX, CH),
            fixed(BLOCKS, ROWS, WIDE, LANES),
            fixed(ROWS, WIDE, LANES),
            fixed(1, CH),
            pl.BlockSpec((8, LANES), lambda j: (0, j)),
            pl.BlockSpec((ROWS, COLS, LANES), lambda j: (0, 0, j)),
        ],
        out_specs=(
            pl.BlockSpec((1, 64, LANES), lambda j: (j, 0, 0)),
            pl.BlockSpec((1, ROWS, WIDE, LANES), lambda j: (j, 0, 0, 0)),
        ),
        scratch_shapes=[
            pltpu.VMEM((20, 24, LANES), F32),
            pltpu.VMEM((BLOCKS, ROWS, WIDE, LANES), F32),
            pltpu.VMEM((49, 8, LANES), F32),
            pltpu.VMEM((BLOCKS, 8, LANES), F32),
        ],
        compiler_params=params(12),
        interpret=INTERPRET,
        name="norm_back",
    )(weight, zero, one, two, three, centred, inv, gain, scale, image)


def input_kernel(conv_ref, kernel_ref, scaled_ref, out_ref, padded):
    @pl.when(pl.program_id(0) == 0)
    def _():
        padded[...] = jnp.zeros_like(padded)

    padded[3:17, 3 : 3 + WIDE, :] = conv_ref[0]
    halves = taps_sum(padded, kernel_ref[...].astype(F32), True)
    for half in range(2):
        rows = slice(half * 7 * WIDE, (half + 1) * 7 * WIDE)
        scaled = scaled_ref[rows, :].astype(F32).reshape(7, WIDE, LANES)
        out_ref[0, half * 7 : half * 7 + 7] = (scaled + halves[half])[:, 0:COLS, :]


def input_grad(conv, kernel, scaled):
    return pl.pallas_call(
        input_kernel,
        grid=(BLOCKS,),
        out_shape=jax.ShapeDtypeStruct((1, ROWS, COLS, CH), F32),
        in_specs=[
            pl.BlockSpec((1, ROWS, WIDE, LANES), lambda j: (j, 0, 0, 0)),
            pl.BlockSpec((49, LANES), lambda j: (0, j)),
            pl.BlockSpec((PIX, LANES), lambda j: (0, j)),
        ],
        out_specs=pl.BlockSpec((1, ROWS, COLS, LANES), lambda j: (0, 0, 0, j)),
        scratch_shapes=[pltpu.VMEM((20, 24, LANES), F32)],
        compiler_params=params(6),
        interpret=INTERPRET,
        name="input_grad",
    )(conv, kernel, scaled)


def finish_kernel(
    images, place_ref, small_in, small_core_in, pre_ref, mine_ref, other_ref,
    image_ref, first_ref, second_ref, bias_ref, kernel_ref, gain_ref, scale_ref, gathered, small_ref,
):
    half, core, column, pair = place_ref[0], place_ref[1], place_ref[2], place_ref[3]
    for b in range(2):
        gathered[b * 2 + core] = mine_ref[:, b]
        gathered[b * 2 + 1 - core] = other_ref[:, b]
    for a in range(2):
        for b in range(2):
            part = 2 * (pair + a - 2 * a * pair) + (half + b - 2 * b * half)
            rows = slice((a * 2 + b) * OWN, (a * 2 + b + 1) * OWN)
            for first, source in ((core, small_in), (1 - core, small_core_in)):
                small_ref[pl.ds(pl.multiple_of((first * 4 + part) * OWN, OWN), OWN), :] = source[rows, :]
    factor = images / small_ref[51:52, :]
    lane = lax.broadcasted_iota(jnp.int32, (8, CH), 1)
    bias = jnp.zeros((8, CH), F32)
    for q in range(4):
        rows = gathered[q, 7, 16:32, :].astype(F32)
        line = jnp.concatenate([rows[k : k + 1, :] for k in range(BLOCKS)], axis=1)
        line = pltpu.roll(jnp.broadcast_to(line, (8, CH)), lax.rem(CH - column * UNITS + q * OWN, CH), 1)
        bias = jnp.where((lane >= q * OWN) & (lane < (q + 1) * OWN), line, bias)
    bias_ref[...] = bias[0:1, 0:192] * jnp.concatenate([factor, factor[:, 0:64]], axis=1)
    for j in range(BLOCKS):
        lanes = slice(j * LANES, (j + 1) * LANES)
        image_ref[0, :, :, lanes] = (pre_ref[0, :, :, lanes] * factor.reshape(1, 1, LANES)).astype(BF16)
        for a in range(7):
            kernel_ref[a, :, lanes] = small_ref[j * 64 + a * 7 : j * 64 + a * 7 + 7, :] * factor
        gain_ref[lanes] = small_ref[j * 64 + 49, :] * factor[0]
        scale_ref[lanes] = small_ref[j * 64 + 50, :] * factor[0]
        for q in range(4):
            for part in range(3):
                rows = slice(q * OWN + part * 16, q * OWN + part * 16 + 16)
                for out_ref, start in ((second_ref, 0), (first_ref, 18)):
                    s = start + j * 3 + part
                    piece = gathered[q, s // 5, (s % 5) * 16 : (s % 5) * 16 + 16, :]
                    out_ref[rows, lanes] = piece.astype(F32) * factor


def finish(images, place, small, small_core, pre, mine, other):
    return pl.pallas_call(
        functools.partial(finish_kernel, images),
        grid=(1,),
        out_shape=(
            jax.ShapeDtypeStruct((1, ROWS, COLS, CH), BF16),
            jax.ShapeDtypeStruct((192, CH), F32),
            jax.ShapeDtypeStruct((192, CH), F32),
            jax.ShapeDtypeStruct((1, 192), F32),
            jax.ShapeDtypeStruct((7, 7, CH), F32),
            jax.ShapeDtypeStruct((CH,), F32),
            jax.ShapeDtypeStruct((CH,), F32),
        ),
        in_specs=[scalars(), block(4 * OWN, LANES), block(4 * OWN, LANES), block(1, ROWS, COLS, CH)]
        + [block(8, 2, 80, LANES)] * 2,
        out_specs=(
            block(1, ROWS, COLS, CH),
            block(192, CH),
            block(192, CH),
            block(1, 192),
            block(7, 7, CH),
            block(CH),
            block(CH),
        ),
        scratch_shapes=[pltpu.VMEM((4, 8, 80, LANES), BF16), pltpu.VMEM((8 * OWN, LANES), F32)],
        compiler_params=params(12),
        interpret=INTERPRET,
        name="finish",
    )(place, small, small_core, pre, mine, other)


def to_all(value, axes):
    count = lax.axis_size(axes)
    return lax.all_to_all(jnp.broadcast_to(value, (count, *value.shape)), axes, 0, 0, tiled=True)


def swap(axis, value):
    return lax.ppermute(value, axis, [(0, 1), (1, 0)])


def swap_core(value):
    return swap("core", value)


def split(small, holds):
    row = lax.broadcasted_iota(jnp.int32, small.shape, 0)
    rest = small - small.astype(BF16).astype(F32)
    return jnp.where((row == 4) & holds, jnp.roll(rest, 1, 0), small).astype(BF16)


def join(small, holds):
    row = lax.broadcasted_iota(jnp.int32, small.shape, 0)
    return jnp.where((row == 3) & holds, small + jnp.roll(small, -1, 0), small)


def ring(value, shift):
    return lax.ppermute(value, RING, [(i, (i + shift) % 4) for i in range(4)])


def ring_share(value):
    return [value] + [ring(value, r) for r in range(1, 4)]


def per_device(
    image, upstream, group_ids, group_weights, conv_kernel, norm_gain, first_weight, first_bias, second_weight, layer_scale
):
    core = lax.axis_index("core")
    half = lax.axis_index("xh")
    column = lax.axis_index("z")
    place = jnp.stack([half * 2 + core, column]).astype(jnp.int32)
    packed = pack_weights(place, first_weight, first_bias, second_weight)
    packed = lax.all_gather(packed, "z", axis=0, tiled=True).reshape(8, 2, PACK, CH)

    kernel = conv_kernel.reshape(49, CH)
    gain = norm_gain.reshape(1, CH)
    layer = layer_scale.reshape(1, CH)
    normed, centred, inv = forward(image[0], kernel, gain)
    normed_all = ring_share(normed)

    labels = jnp.arange(group_weights.shape[0], dtype=jnp.int32)
    own_weight = jnp.sum(jnp.where(labels == group_ids[0], group_weights, 0.0))
    scaled = (own_weight * upstream[0].astype(F32)).astype(BF16)
    scaled = jnp.pad(scaled, ((0, 0), (0, WIDE - COLS), (0, 0))).reshape(PIX, CH)
    scaled_all = ring_share(scaled)

    *parts, grads, scale = hidden(normed_all, scaled_all, packed, layer)
    grads = lax.psum_scatter(grads, "z", scatter_dimension=0, tiled=True).reshape(2, 8, 80, LANES)
    grads = (grads[0].astype(F32) + swap_core(grads[1]).astype(F32)).astype(BF16)

    returned = [ring(parts[r], 4 - r) for r in range(1, 4)]
    small, conv_grad = backward(own_weight.reshape(1), parts[0], *returned, centred, inv, gain, scale, image[0])
    small = lax.all_to_all(small.reshape(8, OWN, LANES), TEAM, 0, 0, tiled=True)
    holds = lax.axis_index(TEAM) == 1
    small = join(jnp.sum(to_all(split(jnp.sum(small, axis=0), holds), "z").astype(F32), axis=0), holds)
    both = jnp.broadcast_to(split(small, holds), (8, OWN, LANES))
    both = lax.all_to_all(jnp.concatenate([grads, both], axis=1), "y", 0, 0, tiled=True).astype(F32)
    mine = to_all(jnp.sum(both[:, 0:80, :], axis=0).astype(BF16), ("y", "xh")).reshape(8, 2, 80, LANES)
    small = join(jnp.sum(both[:, 80:128, :], axis=0), holds)
    small = jnp.concatenate([small, swap("xh", small)], axis=0)
    small = jnp.concatenate([small, swap("xl", small)], axis=0)
    pre = input_grad(conv_grad, kernel, scaled)
    small, mine, pre = lax.optimization_barrier((small, mine, pre))
    images = float(lax.axis_size(REPLICA) * lax.axis_size(SHARD))
    grad_image, grad_first, grad_second, grad_bias, grad_kernel, grad_gain, grad_scale = finish(
        images,
        jnp.stack([half, core, column, lax.axis_index("xl")]).astype(jnp.int32),
        small, swap_core(small), pre, mine, swap_core(mine),
    )
    return (
        grad_image,
        grad_first.T,
        grad_bias.reshape(4 * OWN),
        grad_second,
        grad_kernel,
        grad_gain,
        grad_scale,
    )


def solution(mesh):
    fine = Mesh(mesh.devices.reshape(8, 2, 2, 2, 8), ("y", "xh", "core", "xl", "z"))
    images = P((*REPLICA, *SHARD), None, None, None)
    return jax.shard_map(
        per_device,
        mesh=fine,
        in_specs=(
            images,
            images,
            P((*REPLICA, *SHARD)),
            P(),
            P(),
            P(),
            P(None, SHARD),
            P(SHARD),
            P(SHARD, None),
            P(),
        ),
        out_specs=(images, P(None, SHARD), P(SHARD), P(SHARD, None), P(), P(), P()),
        check_vma=False,
    )
```

```python
import functools

import jax
import jax.numpy as jnp
import numpy as np
from jax import lax
from jax.experimental import pallas as pl
from jax.experimental.pallas import tpu as pltpu
from jax.sharding import Mesh, PartitionSpec as P

F32 = jnp.float32
BF16 = jnp.bfloat16
ROWS = 14
COLS = 14
WIDE = 16
PIX = ROWS * WIDE
CH = 768
LANES = 128
BLOCKS = CH // LANES
OWN = 48
UNITS = 2 * OWN
PACK = UNITS + 16
REPLICA = ("y", "xh", "core")
SHARD = ("xl", "z")
RING = ("xh", "xl")
TEAM = ("core", "xl", "xh")
INTERPRET = False
HIDDEN_MIB = 52


def params(limit_mib, **more):
    return pltpu.CompilerParams(vmem_limit_bytes=limit_mib * 1024 * 1024, **more)


def nt(left, right):
    return lax.dot_general(left, right, (((1,), (1,)), ((), ())), preferred_element_type=F32)


def tn(left, right):
    return lax.dot_general(left, right, (((0,), (0,)), ((), ())), preferred_element_type=F32)


def whole():
    return pl.BlockSpec(memory_space=pltpu.VMEM)


def scalars():
    return pl.BlockSpec(memory_space=pltpu.SMEM)


def block(*shape):
    return pl.BlockSpec(shape, lambda i: (0,) * len(shape))


def pack_kernel(place_ref, first_in, bias_in, second_in, out_ref, bias_ref, sems):
    q = place_ref[0]
    column = place_ref[1]
    blocks = (q, q + 1 - 2 * lax.rem(q, 2))
    copies = [pltpu.make_async_copy(bias_in, bias_ref, sems.at[4])]
    for k in range(2):
        rows = pl.ds(pl.multiple_of(blocks[k] * OWN, OWN), OWN)
        copies.append(pltpu.make_async_copy(first_in.at[rows], out_ref.at[k, pl.ds(0, OWN)], sems.at[k]))
        copies.append(pltpu.make_async_copy(second_in.at[rows], out_ref.at[k, pl.ds(OWN, OWN)], sems.at[2 + k]))
    for copy in copies:
        copy.start()
    copies[0].wait()
    bias = jnp.broadcast_to(bias_ref[...], (16, 192))
    high = bias.astype(BF16)
    low = (bias - high.astype(F32)).astype(BF16)
    bias_row = lax.broadcasted_iota(jnp.int32, (16, 192), 0)
    both = jnp.where(bias_row == 0, high.astype(F32), low.astype(F32)).astype(BF16)
    unit = lax.broadcasted_iota(jnp.int32, (192, CH), 0)
    spot = lax.broadcasted_iota(jnp.int32, (192, CH), 1) - column * UNITS
    for k in range(2):
        put = ((unit == spot + blocks[k] * OWN) & (spot >= 0) & (spot < OWN)).astype(BF16)
        out_ref[k, UNITS:PACK, :] = jnp.dot(both, put, preferred_element_type=F32).astype(BF16)
    for copy in copies[1:]:
        copy.wait()


def pack_weights(place, first_weight, first_bias, second_weight):
    return pl.pallas_call(
        pack_kernel,
        grid=(1,),
        out_shape=jax.ShapeDtypeStruct((2, PACK, CH), BF16),
        in_specs=[scalars()] + [pl.BlockSpec(memory_space=pl.ANY)] * 3,
        out_specs=block(2, PACK, CH),
        scratch_shapes=[
            pltpu.VMEM((1, 192), F32),
            pltpu.SemaphoreType.DMA((5,)),
        ],
        compiler_params=params(58),
        interpret=INTERPRET,
        name="pack",
    )(place, first_weight.T, first_bias.reshape(1, 192), second_weight)


def taps_sum(padded_ref, kernel, flip):
    halves = []
    for half in range(2):
        total = jnp.zeros((7, WIDE, LANES), F32)
        for b in range(7):
            moved = padded_ref[half * 7 : half * 7 + 13, b : b + WIDE, :]
            for a in range(7):
                tap = (6 - a) * 7 + (6 - b) if flip else a * 7 + b
                total = total + moved[a : a + 7] * kernel[tap : tap + 1, :].reshape(1, 1, LANES)
        halves.append(total)
    return halves


def column_mask():
    return (lax.broadcasted_iota(jnp.int32, (ROWS, WIDE, LANES), 1) < COLS).astype(F32)


def forward_kernel(image_ref, kernel_ref, gain_ref, normed_ref, centred_ref, inv_ref, padded, conv):
    j = pl.program_id(0)

    @pl.when(j == 0)
    def _():
        padded[...] = jnp.zeros_like(padded)

    padded[3:17, 3:17, :] = image_ref[...].astype(F32)
    halves = taps_sum(padded, kernel_ref[...].astype(F32), False)
    conv[j, 0:7] = halves[0]
    conv[j, 7:14] = halves[1]

    @pl.when(j == BLOCKS - 1)
    def _():
        mask = column_mask()
        total = conv[0]
        for i in range(1, BLOCKS):
            total = total + conv[i]
        mean = jnp.sum(total, axis=-1, keepdims=True) * (1.0 / CH)
        square = jnp.zeros((ROWS, WIDE, LANES), F32)
        for i in range(BLOCKS):
            part = conv[i] - mean
            square = square + part * part
        inv = lax.rsqrt(jnp.sum(square, axis=-1, keepdims=True) * (1.0 / CH) + 1e-06)
        inv_ref[...] = jnp.broadcast_to(inv, (ROWS, WIDE, LANES))
        for i in range(BLOCKS):
            part = (conv[i] - mean) * inv * mask
            centred_ref[i] = part
            lanes = slice(i * LANES, (i + 1) * LANES)
            gain = gain_ref[:, lanes].reshape(1, 1, LANES)
            normed_ref[:, lanes] = (part * gain).reshape(PIX, LANES).astype(BF16)


def forward(image, kernel, gain):
    return pl.pallas_call(
        forward_kernel,
        grid=(BLOCKS,),
        out_shape=(
            jax.ShapeDtypeStruct((PIX, CH), BF16),
            jax.ShapeDtypeStruct((BLOCKS, ROWS, WIDE, LANES), F32),
            jax.ShapeDtypeStruct((ROWS, WIDE, LANES), F32),
        ),
        in_specs=[
            pl.BlockSpec((ROWS, COLS, LANES), lambda j: (0, 0, j)),
            pl.BlockSpec((49, LANES), lambda j: (0, j)),
            pl.BlockSpec((1, CH), lambda j: (0, 0)),
        ],
        out_specs=(
            pl.BlockSpec((PIX, CH), lambda j: (0, 0)),
            pl.BlockSpec((BLOCKS, ROWS, WIDE, LANES), lambda j: (0, 0, 0, 0)),
            pl.BlockSpec((ROWS, WIDE, LANES), lambda j: (0, 0, 0)),
        ),
        scratch_shapes=[
            pltpu.VMEM((20, 24, LANES), F32),
            pltpu.VMEM((BLOCKS, ROWS, WIDE, LANES), F32),
        ],
        compiler_params=params(8),
        interpret=INTERPRET,
        name="conv_norm",
    )(image, kernel, gain)


def hidden_kernel(*refs):
    normed_in = refs[0:4]
    scaled_in = refs[4:8]
    pack_in, layer_ref = refs[8:10]
    part_outs = refs[10:14]
    grads_out, scale_ref = refs[14:16]
    normed, scaled, firsts, seconds, biases, act, grad, parts, out_ref, slopes, sems, out_sems = refs[16:28]
    first_copies, second_copies, normed_copies, scaled_copies, sends = [], [], [], [], []
    for k in range(2):
        whole_z = pl.ds(0, 8)
        first_copies.append(
            pltpu.make_async_copy(pack_in.at[whole_z, k, pl.ds(0, OWN)], firsts.at[whole_z, k], sems.at[k])
        )
        first_copies.append(
            pltpu.make_async_copy(pack_in.at[whole_z, k, pl.ds(UNITS, 16)], biases.at[k], sems.at[2 + k])
        )
        second_copies.append(
            pltpu.make_async_copy(pack_in.at[whole_z, k, pl.ds(OWN, OWN)], seconds.at[whole_z, k], sems.at[4 + k])
        )
    for i in range(4):
        rows = pl.ds(i * PIX, PIX)
        normed_copies.append(pltpu.make_async_copy(normed_in[i], normed.at[rows], sems.at[6 + i]))
        scaled_copies.append(pltpu.make_async_copy(scaled_in[i], scaled.at[rows], sems.at[10 + i]))
    for copy in [*first_copies, *normed_copies, *second_copies, *scaled_copies]:
        copy.start()
    for copy in first_copies:
        copy.wait()
    first = firsts[...].reshape(CH, CH)
    halves = []
    for k in range(2):
        rows = jnp.sum(biases[k].astype(F32), axis=0)
        halves.append(jnp.broadcast_to(rows[0:1, :] + rows[1:2, :], (8, CH)))
    bias = (halves[0] + pltpu.roll(halves[1], OWN, 1))[0:1, :]
    layer = layer_ref[...]
    for i in range(4):
        rows = slice(i * PIX, (i + 1) * PIX)
        normed_copies[i].wait()
        preact = nt(normed[rows, :], first) + bias
        cumulative = 0.5 * (1.0 + lax.erf(preact * 0.7071067811865476))
        slopes[rows, :] = cumulative + preact * jnp.exp(-0.5 * preact * preact) * 0.3989422804014327
        act[rows, :] = (preact * cumulative).astype(BF16)
    for copy in second_copies:
        copy.wait()
    second = seconds[...].reshape(CH, CH)
    for i in range(4):
        rows = slice(i * PIX, (i + 1) * PIX)
        scaled_copies[i].wait()
        branch_grad = (scaled[rows, :].astype(F32) * layer).astype(BF16)
        preact_grad = (nt(branch_grad, second) * slopes[rows, :]).astype(BF16)
        grad[rows, :] = preact_grad
        parts[rows, :] = jnp.dot(preact_grad, first, preferred_element_type=F32).astype(BF16)
        sends.append(pltpu.make_async_copy(parts.at[pl.ds(i * PIX, PIX)], part_outs[i], out_sems.at[i]))
        sends[-1].start()
    product = tn(act[...], scaled[...])
    scale_ref[...] = jnp.sum((second.astype(F32) * product).reshape(CH // 8, 8, CH), axis=0)
    spread(out_ref, (product * layer).astype(BF16), 0)
    for half in range(2):
        rows = pl.ds(half * 640, 288)
        sends.append(
            pltpu.make_async_copy(
                out_ref.at[pl.ds(0, 8), rows], grads_out.at[pl.ds(0, 8), rows], out_sems.at[4 + half]
            )
        )
        sends[-1].start()
    spread(out_ref, tn(grad[...], normed[...]).astype(BF16), 18)
    bias = jnp.dot(jnp.ones((16, 4 * PIX), BF16), grad[...], preferred_element_type=F32)
    row = lax.broadcasted_iota(jnp.int32, (16, LANES), 0)
    empty = jnp.zeros((16, LANES), BF16)
    for half in range(2):
        if half == 1:
            bias = pltpu.roll(bias, CH - OWN, 1)
        rows = jnp.zeros((16, LANES), F32)
        for k in range(BLOCKS):
            rows = jnp.where(row == k, bias[:, k * LANES : (k + 1) * LANES], rows)
        rows = rows.astype(BF16)
        for z in range(8):
            for s in range(36, 40):
                out_ref[z, half * 640 + s * 16 : half * 640 + s * 16 + 16, :] = rows if s == 36 else empty
        span = pl.ds(half * 640 + 288, 352)
        sends.append(
            pltpu.make_async_copy(
                out_ref.at[pl.ds(0, 8), span], grads_out.at[pl.ds(0, 8), span], out_sems.at[6 + half]
            )
        )
        sends[-1].start()
    for send in sends:
        send.wait()


def spread(out_ref, matrix, start):
    for half in range(2):
        for z in range(8):
            for j in range(BLOCKS):
                for part in range(3):
                    s = start + j * 3 + part
                    row = z * UNITS + half * OWN + part * 16
                    out_ref[z, half * 640 + s * 16 : half * 640 + s * 16 + 16, :] = matrix[
                        row : row + 16, j * LANES : (j + 1) * LANES
                    ]


def hidden(normed, scaled, pack, layer):
    free = pl.BlockSpec(memory_space=pl.ANY)
    return pl.pallas_call(
        hidden_kernel,
        grid=(1,),
        out_shape=(jax.ShapeDtypeStruct((PIX, CH), BF16),) * 4
        + (jax.ShapeDtypeStruct((8, 1280, LANES), BF16),)
        + (jax.ShapeDtypeStruct((8, CH), F32),),
        in_specs=[free] * 9 + [block(1, CH)],
        out_specs=(free,) * 5 + (block(8, CH),),
        scratch_shapes=[
            pltpu.VMEM((4 * PIX, CH), BF16),
            pltpu.VMEM((4 * PIX, CH), BF16),
            pltpu.VMEM((8, 2, OWN, CH), BF16),
            pltpu.VMEM((8, 2, OWN, CH), BF16),
            pltpu.VMEM((2, 8, 16, CH), BF16),
            pltpu.VMEM((4 * PIX, CH), BF16),
            pltpu.VMEM((4 * PIX, CH), BF16),
            pltpu.VMEM((4 * PIX, CH), BF16),
            pltpu.VMEM((8, 1280, LANES), BF16),
            pltpu.VMEM((4 * PIX, CH), F32),
            pltpu.SemaphoreType.DMA((14,)),
            pltpu.SemaphoreType.DMA((8,)),
        ],
        compiler_params=params(HIDDEN_MIB),
        interpret=INTERPRET,
        name="hidden",
    )(*normed, *scaled, pack, layer)


def backward_kernel(
    weight_ref, zero_ref, one_ref, two_ref, three_ref, centred_ref, inv_ref, gain_ref, scale_ref, image_ref,
    sums_ref, conv_ref, padded, conv, parts, gains,
):
    j = pl.program_id(0)

    @pl.when(j == 0)
    def _():
        padded[...] = jnp.zeros_like(padded)
        first = jnp.zeros((ROWS, WIDE, LANES), F32)
        second = jnp.zeros((ROWS, WIDE, LANES), F32)
        for i in range(BLOCKS):
            lanes = slice(i * LANES, (i + 1) * LANES)
            grad = (
                zero_ref[:, lanes].astype(F32)
                + one_ref[:, lanes].astype(F32)
                + two_ref[:, lanes].astype(F32)
                + three_ref[:, lanes].astype(F32)
            ).reshape(ROWS, WIDE, LANES)
            centred = centred_ref[i]
            product = grad * centred
            gains[i] = jnp.sum(jnp.sum(product, axis=0).reshape(2, 8, LANES), axis=0)
            gain = gain_ref[:, lanes].reshape(1, 1, LANES)
            gained = grad * gain
            conv[i] = gained
            first = first + gained
            second = second + product * gain
        mean = jnp.sum(first, axis=-1, keepdims=True) * (1.0 / CH)
        slant = jnp.sum(second, axis=-1, keepdims=True) * (1.0 / CH)
        inv = inv_ref[...] * column_mask()
        for i in range(BLOCKS):
            conv[i] = inv * (conv[i] - mean - centred_ref[i] * slant)

    padded[3:17, 3:17, :] = image_ref[...].astype(F32)
    conv_ref[0] = conv[j]
    for half in range(2):
        signal = conv[j, half * 7 : half * 7 + 7]
        for b in range(7):
            moved = padded[half * 7 : half * 7 + 13, b : b + WIDE, :]
            for a in range(7):
                product = jnp.sum(signal * moved[a : a + 7], axis=0)
                product = product[0:8] + product[8:16]
                if half == 0:
                    parts[a * 7 + b] = product
                else:
                    parts[a * 7 + b] += product
    sums_ref[0] = jnp.zeros((64, LANES), F32)
    sums_ref[0, 0:49, :] = jnp.sum(parts[...], axis=1)
    sums_ref[0, 49:50, :] = jnp.sum(gains[j], axis=0, keepdims=True)
    sums_ref[0, 50:51, :] = jnp.sum(scale_ref[...], axis=0, keepdims=True)
    sums_ref[0, 51:52, :] = jnp.full((1, LANES), weight_ref[0], F32)


def backward(weight, zero, one, two, three, centred, inv, gain, scale, image):
    def fixed(*shape):
        return pl.BlockSpec(shape, lambda j: (0,) * len(shape))

    return pl.pallas_call(
        backward_kernel,
        grid=(BLOCKS,),
        out_shape=(
            jax.ShapeDtypeStruct((BLOCKS, 64, LANES), F32),
            jax.ShapeDtypeStruct((BLOCKS, ROWS, WIDE, LANES), F32),
        ),
        in_specs=[
            scalars(),
            fixed(PIX, CH),
            fixed(PIX, CH),
            fixed(PIX, CH),
            fixed(PIX, CH),
            fixed(BLOCKS, ROWS, WIDE, LANES),
            fixed(ROWS, WIDE, LANES),
            fixed(1, CH),
            pl.BlockSpec((8, LANES), lambda j: (0, j)),
            pl.BlockSpec((ROWS, COLS, LANES), lambda j: (0, 0, j)),
        ],
        out_specs=(
            pl.BlockSpec((1, 64, LANES), lambda j: (j, 0, 0)),
            pl.BlockSpec((1, ROWS, WIDE, LANES), lambda j: (j, 0, 0, 0)),
        ),
        scratch_shapes=[
            pltpu.VMEM((20, 24, LANES), F32),
            pltpu.VMEM((BLOCKS, ROWS, WIDE, LANES), F32),
            pltpu.VMEM((49, 8, LANES), F32),
            pltpu.VMEM((BLOCKS, 8, LANES), F32),
        ],
        compiler_params=params(12),
        interpret=INTERPRET,
        name="norm_back",
    )(weight, zero, one, two, three, centred, inv, gain, scale, image)


def input_kernel(conv_ref, kernel_ref, scaled_ref, out_ref, padded):
    @pl.when(pl.program_id(0) == 0)
    def _():
        padded[...] = jnp.zeros_like(padded)

    padded[3:17, 3 : 3 + WIDE, :] = conv_ref[0]
    halves = taps_sum(padded, kernel_ref[...].astype(F32), True)
    for half in range(2):
        rows = slice(half * 7 * WIDE, (half + 1) * 7 * WIDE)
        scaled = scaled_ref[rows, :].astype(F32).reshape(7, WIDE, LANES)
        out_ref[0, half * 7 : half * 7 + 7] = (scaled + halves[half])[:, 0:COLS, :]


def input_grad(conv, kernel, scaled):
    return pl.pallas_call(
        input_kernel,
        grid=(BLOCKS,),
        out_shape=jax.ShapeDtypeStruct((1, ROWS, COLS, CH), F32),
        in_specs=[
            pl.BlockSpec((1, ROWS, WIDE, LANES), lambda j: (j, 0, 0, 0)),
            pl.BlockSpec((49, LANES), lambda j: (0, j)),
            pl.BlockSpec((PIX, LANES), lambda j: (0, j)),
        ],
        out_specs=pl.BlockSpec((1, ROWS, COLS, LANES), lambda j: (0, 0, 0, j)),
        scratch_shapes=[pltpu.VMEM((20, 24, LANES), F32)],
        compiler_params=params(6),
        interpret=INTERPRET,
        name="input_grad",
    )(conv, kernel, scaled)


def finish_kernel(
    images, place_ref, small_in, small_core_in, pre_ref, mine_ref, other_ref,
    image_ref, first_ref, second_ref, bias_ref, kernel_ref, gain_ref, scale_ref, gathered, small_ref,
):
    half, core, column, pair = place_ref[0], place_ref[1], place_ref[2], place_ref[3]
    for b in range(2):
        gathered[b * 2 + core] = mine_ref[:, b]
        gathered[b * 2 + 1 - core] = other_ref[:, b]
    for a in range(2):
        for b in range(2):
            part = 2 * (pair + a - 2 * a * pair) + (half + b - 2 * b * half)
            rows = slice((a * 2 + b) * OWN, (a * 2 + b + 1) * OWN)
            for first, source in ((core, small_in), (1 - core, small_core_in)):
                small_ref[pl.ds(pl.multiple_of((first * 4 + part) * OWN, OWN), OWN), :] = source[rows, :]
    factor = images / small_ref[51:52, :]
    lane = lax.broadcasted_iota(jnp.int32, (8, CH), 1)
    bias = jnp.zeros((8, CH), F32)
    for q in range(4):
        rows = gathered[q, 7, 16:32, :].astype(F32)
        line = jnp.concatenate([rows[k : k + 1, :] for k in range(BLOCKS)], axis=1)
        line = pltpu.roll(jnp.broadcast_to(line, (8, CH)), lax.rem(CH - column * UNITS + q * OWN, CH), 1)
        bias = jnp.where((lane >= q * OWN) & (lane < (q + 1) * OWN), line, bias)
    bias_ref[...] = bias[0:1, 0:192] * jnp.concatenate([factor, factor[:, 0:64]], axis=1)
    for j in range(BLOCKS):
        lanes = slice(j * LANES, (j + 1) * LANES)
        image_ref[0, :, :, lanes] = (pre_ref[0, :, :, lanes] * factor.reshape(1, 1, LANES)).astype(BF16)
        for a in range(7):
            kernel_ref[a, :, lanes] = small_ref[j * 64 + a * 7 : j * 64 + a * 7 + 7, :] * factor
        gain_ref[lanes] = small_ref[j * 64 + 49, :] * factor[0]
        scale_ref[lanes] = small_ref[j * 64 + 50, :] * factor[0]
        for q in range(4):
            for part in range(3):
                rows = slice(q * OWN + part * 16, q * OWN + part * 16 + 16)
                for out_ref, start in ((second_ref, 0), (first_ref, 18)):
                    s = start + j * 3 + part
                    piece = gathered[q, s // 5, (s % 5) * 16 : (s % 5) * 16 + 16, :]
                    out_ref[rows, lanes] = piece.astype(F32) * factor


def finish(images, place, small, small_core, pre, mine, other):
    return pl.pallas_call(
        functools.partial(finish_kernel, images),
        grid=(1,),
        out_shape=(
            jax.ShapeDtypeStruct((1, ROWS, COLS, CH), BF16),
            jax.ShapeDtypeStruct((192, CH), F32),
            jax.ShapeDtypeStruct((192, CH), F32),
            jax.ShapeDtypeStruct((1, 192), F32),
            jax.ShapeDtypeStruct((7, 7, CH), F32),
            jax.ShapeDtypeStruct((CH,), F32),
            jax.ShapeDtypeStruct((CH,), F32),
        ),
        in_specs=[scalars(), block(4 * OWN, LANES), block(4 * OWN, LANES), block(1, ROWS, COLS, CH)]
        + [block(8, 2, 80, LANES)] * 2,
        out_specs=(
            block(1, ROWS, COLS, CH),
            block(192, CH),
            block(192, CH),
            block(1, 192),
            block(7, 7, CH),
            block(CH),
            block(CH),
        ),
        scratch_shapes=[pltpu.VMEM((4, 8, 80, LANES), BF16), pltpu.VMEM((8 * OWN, LANES), F32)],
        compiler_params=params(12),
        interpret=INTERPRET,
        name="finish",
    )(place, small, small_core, pre, mine, other)


def to_all(value, axes):
    count = lax.axis_size(axes)
    return lax.all_to_all(jnp.broadcast_to(value, (count, *value.shape)), axes, 0, 0, tiled=True)


def swap(axis, value):
    return lax.ppermute(value, axis, [(0, 1), (1, 0)])


def swap_core(value):
    return swap("core", value)


def split(small, holds):
    row = lax.broadcasted_iota(jnp.int32, small.shape, 0)
    rest = small - small.astype(BF16).astype(F32)
    return jnp.where((row == 4) & holds, jnp.roll(rest, 1, 0), small).astype(BF16)


def join(small, holds):
    row = lax.broadcasted_iota(jnp.int32, small.shape, 0)
    return jnp.where((row == 3) & holds, small + jnp.roll(small, -1, 0), small)


def ring(value, shift):
    return lax.ppermute(value, RING, [(i, (i + shift) % 4) for i in range(4)])


def ring_share(value):
    return [value] + [ring(value, r) for r in range(1, 4)]


def per_device(
    image, upstream, group_ids, group_weights, conv_kernel, norm_gain, first_weight, first_bias, second_weight, layer_scale
):
    core = lax.axis_index("core")
    half = lax.axis_index("xh")
    column = lax.axis_index("z")
    place = jnp.stack([half * 2 + core, column]).astype(jnp.int32)
    packed = pack_weights(place, first_weight, first_bias, second_weight)
    packed = lax.all_gather(packed, "z", axis=0, tiled=True).reshape(8, 2, PACK, CH)

    kernel = conv_kernel.reshape(49, CH)
    gain = norm_gain.reshape(1, CH)
    layer = layer_scale.reshape(1, CH)
    normed, centred, inv = forward(image[0], kernel, gain)
    normed_all = ring_share(normed)

    labels = jnp.arange(group_weights.shape[0], dtype=jnp.int32)
    own_weight = jnp.sum(jnp.where(labels == group_ids[0], group_weights, 0.0))
    scaled = (own_weight * upstream[0].astype(F32)).astype(BF16)
    scaled = jnp.pad(scaled, ((0, 0), (0, WIDE - COLS), (0, 0))).reshape(PIX, CH)
    scaled_all = ring_share(scaled)

    *parts, grads, scale = hidden(normed_all, scaled_all, packed, layer)
    grads = lax.psum_scatter(grads, "z", scatter_dimension=0, tiled=True).reshape(2, 8, 80, LANES)
    grads = (grads[0].astype(F32) + swap_core(grads[1]).astype(F32)).astype(BF16)

    returned = [ring(parts[r], 4 - r) for r in range(1, 4)]
    small, conv_grad = backward(own_weight.reshape(1), parts[0], *returned, centred, inv, gain, scale, image[0])
    small = lax.all_to_all(small.reshape(8, OWN, LANES), TEAM, 0, 0, tiled=True)
    holds = lax.axis_index(TEAM) == 1
    small = join(jnp.sum(to_all(split(jnp.sum(small, axis=0), holds), "z").astype(F32), axis=0), holds)
    both = jnp.broadcast_to(split(small, holds), (8, OWN, LANES))
    both = lax.all_to_all(jnp.concatenate([grads, both], axis=1), "y", 0, 0, tiled=True).astype(F32)
    mine = to_all(jnp.sum(both[:, 0:80, :], axis=0).astype(BF16), ("y", "xh")).reshape(8, 2, 80, LANES)
    small = join(jnp.sum(both[:, 80:128, :], axis=0), holds)
    small = jnp.concatenate([small, swap("xh", small)], axis=0)
    small = jnp.concatenate([small, swap("xl", small)], axis=0)
    pre = input_grad(conv_grad, kernel, scaled)
    small, mine, pre = lax.optimization_barrier((small, mine, pre))
    images = float(lax.axis_size(REPLICA) * lax.axis_size(SHARD))
    grad_image, grad_first, grad_second, grad_bias, grad_kernel, grad_gain, grad_scale = finish(
        images,
        jnp.stack([half, core, column, lax.axis_index("xl")]).astype(jnp.int32),
        small, swap_core(small), pre, mine, swap_core(mine),
    )
    return (
        grad_image,
        grad_first.T,
        grad_bias.reshape(4 * OWN),
        grad_second,
        grad_kernel,
        grad_gain,
        grad_scale,
    )


def solution(mesh):
    fine = Mesh(mesh.devices.reshape(8, 2, 2, 2, 8), ("y", "xh", "core", "xl", "z"))
    images = P((*REPLICA, *SHARD), None, None, None)
    return jax.shard_map(
        per_device,
        mesh=fine,
        in_specs=(
            images,
            images,
            P((*REPLICA, *SHARD)),
            P(),
            P(),
            P(),
            P(None, SHARD),
            P(SHARD),
            P(SHARD, None),
            P(),
        ),
        out_specs=(images, P(None, SHARD), P(SHARD), P(SHARD, None), P(), P(), P()),
        check_vma=False,
    )
```
